256 devices in a mesh: grp: 8 (over z), tm: 32 (over x, y, core).
Axes of the slice: x: 4, y: 4, z: 8, core: 2. Of those that a mesh axis runs over, the one named last changes fastest.
Arguments:
- initial_state: float32 [256, 256], replicated, may hold values from -6 to 6
- retain: float32 [2048, 256], P(('grp', 'tm')), may hold values from 0 to 1
- coupling: float32 [2048, 256, 256], P(('grp', 'tm')), may hold values from -1 to 1
- probe: float32 [256], replicated, may hold values from -0.375 to 0.375
- rec_sample: int32 [256, 32, 16], P(('grp', 'tm')), may hold values from 0 to 255
- rec_step: int32 [256, 32, 16], P(('grp', 'tm')), may hold values from 0 to 7
- rec_count: int32 [256, 32], P(('grp', 'tm')), may hold values from 0 to 16, as said below
- rec_load: float32 [256, 32, 16, 256], P(('grp', 'tm')), may hold values from -1.5 to 1.5
Outputs:
- observed: float32 [2048, 256], P(('grp', 'tm'))
- slice_end: float32 [256, 256, 256], P(('grp', 'tm'))
The draws below stay inside these ranges and needn't reach their ends.
Inputs may be any that keep to these rules, and one draw needn't show every extreme that they name: `rec_count`: A live slot count; in every draw some slice fills all 16 slots to some owner.
All inputs are finite; a program needn't handle non-finite values.
Results may differ from the reference program's by a relative error of at most 0.0003.
Values sent between devices are 32-bit elements; how exact they have to be, the bound alone decides.
No kernel may reach another device: no remote copies, remote signals or barrier semaphores. Data moves between devices by JAX's collectives and lax.ppermute only.
A program may use at most 384 MiB of HBM per device.

```python
import math
import jax
import jax.numpy as jnp
from jax import lax

M = 256
S = 256
TS = 8
CAP = 16
OWNERS = 32
SLICES = 256
HORIZON_LENGTH = 2048
N_GRP = 8
N_TM = 32


def draw_rec_count(key, part):
    counts = jax.random.randint(key, (SLICES, OWNERS), 0, CAP + 1, dtype=jnp.int32)
    chosen = jax.random.randint(jax.random.fold_in(key, 7), (), 0, SLICES * OWNERS, dtype=jnp.int32)
    flat = counts.reshape(-1)
    flat = jnp.where(jnp.arange(SLICES * OWNERS, dtype=jnp.int32) == chosen, CAP, flat)
    return flat.reshape(SLICES, OWNERS)


def draw_retain(key, part):
    key_kind = jax.random.fold_in(key, 11)
    key_slow = jax.random.fold_in(key, 12)
    key_fast = jax.random.fold_in(key, 13)
    key_rough = jax.random.fold_in(key, 14)
    random_seed_spot = jax.random.fold_in(key, 15)
    key_loss = jax.random.fold_in(key, 16)
    share = 0.5
    fast = jax.random.uniform(key_kind, (M,), jnp.float32) < share
    slow_rate = jnp.exp(jax.random.uniform(key_slow, (M,), jnp.float32, math.log(0.05), math.log(0.5))) / HORIZON_LENGTH
    fast_rate = jnp.exp(jax.random.uniform(key_fast, (M,), jnp.float32, math.log(0.06), math.log(0.12)))
    rate = jnp.where(fast, fast_rate, slow_rate) + 1.0 / HORIZON_LENGTH
    rough = jnp.exp(jax.random.uniform(key_rough, (HORIZON_LENGTH, M), jnp.float32, math.log(0.5), math.log(2.0)))
    survival_selector = jnp.exp(-rate[None, :] * rough)
    impact_span_number = jax.random.randint(random_seed_spot, (3,), 0, HORIZON_LENGTH, dtype=jnp.int32)
    node_ordinal = jnp.arange(HORIZON_LENGTH, dtype=jnp.int32)
    impact_active = jnp.any(node_ordinal[:, None] == impact_span_number[None, :], axis=1)
    energy_penalty = jax.random.uniform(key_loss, (HORIZON_LENGTH, M), jnp.float32, 0.5, 0.8)
    survival_selector = jnp.where(impact_active[:, None], survival_selector * energy_penalty, survival_selector)
    return survival_selector.astype(jnp.float32)


def draw_coupling(key, part):
    spread = 5.0 * (4.0 * M * HORIZON_LENGTH) ** (-0.5)
    inner_key = jax.random.fold_in(key, 21)
    values = jnp.clip(jax.random.normal(inner_key, (HORIZON_LENGTH, M, M), jnp.float32), -4.0, 4.0)
    return (values * spread).astype(jnp.float32)


def plant(result, stream_key, low, top_value):
    index_at = [jax.random.randint(jax.random.fold_in(stream_key, axis), (), 0, length) for axis, length in enumerate(result.shape)]
    main_axis = result.shape.index(max(result.shape))
    next_to = index_at[:main_axis] + [(index_at[main_axis] + 1) % result.shape[main_axis]] + index_at[main_axis + 1:]
    return result.at[tuple(index_at)].set(low).at[tuple(next_to)].set(top_value)


def steps_of(stream_key, shape, pieces, least, top_value):
    factor_of, own = 1.0, jax.random.fold_in(stream_key, 6)
    for position, shards_of in pieces:
        draws = jnp.exp(jax.random.uniform(jax.random.fold_in(own, position), (shards_of,), jnp.float32, least / len(pieces), top_value / len(pieces)))
        factor_of = factor_of * jnp.repeat(draws, shape[position] // shards_of).reshape([-1 if axis == position else 1 for axis in range(len(shape))])
    return factor_of


def normal_values(key, dims, scale, reach, cuts=(), held_as=jnp.bfloat16):
    drawn = jax.random.normal(key, dims, jnp.float32) * scale
    if len(cuts) > 0:
        drawn = steps_of(key, dims, cuts, -0.22, 0.18) * drawn
    return jnp.clip(drawn, min=-reach, max=reach).astype(held_as)


def setup_inputs(seed: int = 0) -> dict:
    seeds = jax.random.split(jax.random.key(seed), 9)
    initial_state = normal_values(seeds[0], (S, M), 1.0, 6.0, (), jnp.float32)
    retain = draw_retain(jax.random.fold_in(seeds[8], 71), 0)
    coupling = draw_coupling(jax.random.fold_in(seeds[8], 71), 0)
    probe = normal_values(seeds[3], (M,), M ** -0.5, 0.375, (), jnp.float32)
    rec_sample = plant(jax.random.randint(seeds[4], (SLICES, OWNERS, CAP), 0, S), jax.random.fold_in(seeds[4], 1), 0, S - 1).astype(jnp.int32)
    rec_step = plant(jax.random.randint(seeds[5], (SLICES, OWNERS, CAP), 0, TS), jax.random.fold_in(seeds[5], 1), 0, TS - 1).astype(jnp.int32)
    rec_count = draw_rec_count(jax.random.fold_in(seeds[8], 71), 0)
    rec_load = normal_values(seeds[7], (SLICES, OWNERS, CAP, M), 0.1, 1.5, ((0, 256),), jnp.float32)
    return dict(initial_state=initial_state, retain=retain, coupling=coupling, probe=probe, rec_sample=rec_sample, rec_step=rec_step, rec_count=rec_count, rec_load=rec_load)


def regroup(array):
    rest = array.shape[3:]
    array = array.reshape((N_GRP, N_TM, N_TM, CAP) + rest)
    array = jnp.swapaxes(array, 1, 2)
    return array.reshape((N_GRP * N_TM, N_TM * CAP) + rest)


def reference(initial_state, retain, coupling, probe, rec_sample, rec_step, rec_count, rec_load):
    slices = N_GRP * N_TM
    slot = jnp.arange(CAP, dtype=jnp.int32)
    valid = slot[None, None, :] < rec_count[:, :, None]
    loads = jnp.where(valid[..., None], rec_load, jnp.float32(0.0))
    codes = rec_step * S + rec_sample
    loads = regroup(loads)
    codes = regroup(codes)
    eye = jnp.eye(M, dtype=jnp.float32)
    forwards = jnp.swapaxes(coupling, 1, 2) + eye[None] * retain[:, None, :]
    forwards = forwards.reshape(slices, TS, M, M)

    def one_slice(state, items):
        forward_set, load_rows, code_rows = items
        impulse = jnp.zeros((TS * S, M), jnp.float32).at[code_rows].add(load_rows).reshape(TS, S, M)

        def one_step(field, inner):
            forward, kick = inner
            field = jnp.dot(field, forward, precision=lax.Precision.HIGHEST, preferred_element_type=jnp.float32) + kick
            return field, jnp.dot(field, probe, precision=lax.Precision.HIGHEST)

        state, seen = lax.scan(one_step, state, (forward_set, impulse))
        return state, (seen, state)

    final, (seen, ends) = lax.scan(one_slice, initial_state, (forwards, loads, codes))
    return seen.reshape(HORIZON_LENGTH, S), ends
```

```python
import functools

import jax
import jax.numpy as jnp
from jax import lax
from jax.experimental import pallas as pl
from jax.experimental.pallas import tpu as pltpu
from jax.sharding import PartitionSpec as P

F32 = jnp.float32
BF16 = jnp.bfloat16
NY = 4
NX = 4
SHIFTS = (1, 3, 2)


def split(a):
    hi = a.astype(BF16)
    return hi, (a - hi.astype(F32)).astype(BF16)


def dot(a, b, transposed=False):
    dims = (((1,), (1 if transposed else 0,)), ((), ()))
    return lax.dot_general(a, b, dims, preferred_element_type=F32)


def mm(left, right, transposed=False):
    ah, al = left
    bh, bl = right
    return dot(ah, bh, transposed) + (dot(ah, bl, transposed) + dot(al, bh, transposed))


def call(kernel, name, outs, *args, scratch=(), flops=0):
    shapes = [jax.ShapeDtypeStruct(s, F32) for s in outs]
    smem = pl.BlockSpec(memory_space=pltpu.SMEM)
    vmem = pl.BlockSpec(memory_space=pltpu.VMEM)
    moved = sum(4 * a.size for a in args) + sum(4 * s.size for s in shapes)
    return pl.pallas_call(
        kernel,
        out_shape=shapes,
        in_specs=[smem] + [vmem] * (len(args) - 1),
        out_specs=[vmem] * len(shapes),
        scratch_shapes=list(scratch),
        name=name,
        cost_estimate=pl.CostEstimate(flops=flops, bytes_accessed=moved, transcendentals=0),
        compiler_params=pltpu.CompilerParams(vmem_limit_bytes=32 * 1024 * 1024),
    )(*args)


def compose_kernel(pos, retain, coupling, whole):
    steps, modes = retain.shape
    rows = lax.broadcasted_iota(jnp.int32, (modes, modes), 0)
    cols = lax.broadcasted_iota(jnp.int32, (modes, modes), 1)
    total = coupling[0].T + jnp.where(rows == cols, retain[0:1, :], 0.0)
    for t in range(1, steps):
        total = total * retain[t : t + 1, :] + mm(split(total), split(coupling[t]), True)
    whole[...] = total


def weights_kernel(pos, retain, coupling, probe, seen):
    steps, modes = retain.shape
    rows = lax.broadcasted_iota(jnp.int32, (steps, modes), 0)
    state = jnp.zeros((steps, modes), F32)
    for t in range(steps - 1, -1, -1):
        state = jnp.where(rows == t, probe[...], state)
        state = state * retain[t : t + 1, :] + mm(split(state), split(coupling[t]))
    seen[...] = state


def drive_kernel(pos, arrived, retain, coupling, probe, shifted, kept, sent, seen):
    steps, modes = retain.shape
    sources, half, _ = arrived.shape
    n = sources * half
    samples = shifted.shape[0]
    loads = jnp.concatenate(
        [
            arrived[:, :, 0:modes].reshape(n, modes),
            arrived[:, :, modes : 2 * modes].reshape(n, modes),
        ],
        axis=0,
    )
    lh, ll = split(loads)
    codes = arrived[:, :, 2 * modes : 2 * modes + 128].reshape(n, 128).T
    codes = jnp.concatenate([codes[0:1, :], codes[1:2, :]], axis=1).astype(jnp.int32)
    place = lax.broadcasted_iota(jnp.int32, (samples, 2 * n), 0)
    ph, pw = split(jnp.broadcast_to(probe[...], (8, modes)))
    rows = lax.broadcasted_iota(jnp.int32, (8, samples), 0)
    shown = jnp.zeros((8, samples), F32)
    field = None
    for t in range(steps):
        hit = jnp.where(place + t * samples == codes, 1.0, 0.0).astype(BF16)
        kick = dot(hit, lh) + dot(hit, ll)
        if t > 0:
            kick = kick + field * retain[t : t + 1, :] + mm(parts, split(coupling[t]), True)
        field = kick
        parts = split(field)
        shown = jnp.where(rows == t, mm((ph, pw), parts, True), shown)
    shifted[...] = field
    seen[...] = shown
    c = pos[0]
    h = samples // 2

    @pl.when(c == 0)
    def _():
        kept[...] = field[:h]
        sent[...] = field[h:]

    @pl.when(c != 0)
    def _():
        kept[...] = field[h:]
        sent[...] = field[:h]


def pair_kernel(pos, mine, other, both, chip):
    c = pos[0]

    @pl.when(c == 0)
    def _():
        both[0] = mine[...]
        both[1] = other[...]

    @pl.when(c != 0)
    def _():
        both[0] = other[...]
        both[1] = mine[...]

    chip[...] = mm(split(both[0]), split(both[1]))


def order(place, count, ordered, refs):
    ordered[place] = refs[0][...]
    for s, ref in zip(SHIFTS, refs[1:]):
        ordered[lax.rem(place + count - s, count)] = ref[...]


def line_map_kernel(pos, a0, a1, a3, a2, ordered, prefix, line):
    order(pos[1], NY, ordered, (a0, a1, a3, a2))
    total = ordered[0]
    for k in range(1, NY):
        prefix[k - 1] = total
        total = mm(split(total), split(ordered[k]))
    line[...] = total


def group_map_kernel(pos, a0, a1, a3, a2, prefix, ordered, through, group, before):
    x = pos[2]
    order(x, NX, ordered, (a0, a1, a3, a2))
    modes = group.shape[0]
    rows = lax.broadcasted_iota(jnp.int32, (modes, modes), 0)
    cols = lax.broadcasted_iota(jnp.int32, (modes, modes), 1)
    before[0] = jnp.where(rows == cols, 1.0, 0.0)
    total = ordered[0]
    for k in range(1, NX):
        before[k] = total
        total = mm(split(total), split(ordered[k]))
    group[...] = total
    own = before[x]
    through[0] = own
    own = split(own)
    for k in range(1, NY):
        through[k] = mm(own, split(prefix[k - 1]))


def product_kernel(pos, left, right, out):
    out[...] = mm(split(left[...]), split(right[...]))


def pair_shift_kernel(pos, kept, got, both, first, s0, s1, s3, s2, chip):
    c = pos[0]
    y = pos[1]
    r = s0.shape[0]
    mine = kept[...]
    theirs = got[...]
    zero = jnp.where(c == 0, mine, theirs)
    one = jnp.where(c == 0, theirs, mine)
    first[...] = zero
    chip[...] = mm(split(zero), split(both[1])) + one
    for s, out in zip((0,) + SHIFTS, (s0, s1, s3, s2)):
        start = pl.multiple_of(lax.rem(y + s, NY) * r, r)
        out[...] = chip[pl.ds(start, r), :]


def line_shift_kernel(pos, b0, b1, b3, b2, maps, before, line, ordered):
    order(pos[1], NY, ordered, (b0, b1, b3, b2))
    total = ordered[0]
    for k in range(1, NY):
        before[k - 1] = total
        total = mm(split(total), split(maps[k])) + ordered[k]
    line[...] = total


def group_shift_kernel(pos, b0, b1, b3, b2, maps, prefix, before, through, group, ordered, own):
    x = pos[2]
    order(x, NX, ordered, (b0, b1, b3, b2))
    own[0] = jnp.zeros_like(ordered[0])
    total = ordered[0]
    for k in range(1, NX):
        own[k] = total
        total = mm(split(total), split(maps[k])) + ordered[k]
    group[...] = total
    prior = own[x]
    through[0] = prior
    prior = split(prior)
    for k in range(1, NY):
        through[k] = mm(prior, split(prefix[k - 1])) + before[k - 1]


def first_hop_kernel(pos, initial, got1, got2, before, out):
    c, y, g = pos[0], pos[1], pos[3]
    r = out.shape[0]
    start = pl.multiple_of(c * (NY * r) + y * r, r)
    released = initial[pl.ds(start, r), :]
    near = jnp.where(g == 0, released, got1[...])
    far = jnp.where(g == 1, released, got2[...])
    far = jnp.where(g == 0, 0.0, far)
    out[...] = near + mm(split(far), split(before[...]))


def hop_kernel(pos, mine, got, before, out):
    out[...] = mine[...] + mm(split(got[...]), split(before[...]))


def last_hop_kernel(pos, mine, got, before, maps, shifts, s0, s1, s3, s2, chips):
    y = pos[1]
    group = split(mine[...] + mm(split(got[...]), split(before[...])))
    for k in range(NY):
        chips[k] = mm(group, split(maps[k])) + shifts[k]
    for s, out in zip((0,) + SHIFTS, (s0, s1, s3, s2)):
        out[...] = chips[lax.rem(y + s, NY)]


def chip_kernel(pos, e0, e1, e3, e2, both, first, kept, sent, chip):
    c, y = pos[0], pos[1]
    r = e0.shape[0]
    for s, ref in zip((0,) + SHIFTS, (e0, e1, e3, e2)):
        start = pl.multiple_of(lax.rem(y + NY - s, NY) * r, r)
        chip[pl.ds(start, r), :] = ref[...]
    zero = chip[...]
    one = mm(split(zero), split(both[0])) + first[...]
    kept[...] = jnp.where(c == 0, zero, one)
    sent[...] = jnp.where(c == 0, one, zero)


def finish_kernel(pos, kept, got, whole, shifted, weights, driven, observed, final, start):
    c = pos[0]
    h = kept.shape[0]

    @pl.when(c == 0)
    def _():
        start[:h] = kept[...]
        start[h:] = got[...]

    @pl.when(c != 0)
    def _():
        start[:h] = got[...]
        start[h:] = kept[...]

    parts = split(start[...])
    final[...] = mm(parts, split(whole[...])) + shifted[...]
    observed[...] = mm(split(weights[...]), parts, True) + driven[...]


def body(initial_state, retain, coupling, probe, rec_sample, rec_step, rec_count, rec_load):
    steps, modes, _ = coupling.shape
    samples = initial_state.shape[0]
    owners, cap = rec_sample.shape[1:]
    half = samples // 2
    part = half // NY
    mat = (modes, modes)
    vm = lambda *s: pltpu.VMEM(s, F32)

    t = lax.axis_index("tm")
    g = lax.axis_index("grp")
    pos = jnp.stack([t % 2, (t // 2) % NY, t // (2 * NY), g]).astype(jnp.int32)

    def at(x, y, c):
        return (x * NY + y) * 2 + c

    spots = [(x, y, c) for x in range(NX) for y in range(NY) for c in range(2)]
    swap = [(at(x, y, c), at(x, y, 1 - c)) for x, y, c in spots]

    def along_y(s):
        return [(at(x, y, c), at(x, (y + s) % NY, c)) for x, y, c in spots]

    def along_x(s):
        return [(at(x, y, c), at((x + s) % NX, y, c)) for x, y, c in spots]

    n_grp = lax.axis_size("grp")

    def later(a, s):
        return lax.ppermute(a, "grp", [(i, i + s) for i in range(n_grp - s)])

    slot = lax.broadcasted_iota(jnp.int32, rec_sample.shape, 2)
    codes = jnp.where(slot < rec_count[:, :, None], rec_step * samples + rec_sample, -1)
    codes = codes[0].astype(F32)
    lane = lax.broadcasted_iota(jnp.int32, (owners, cap // 2, 128), 2)
    tags = jnp.where(
        lane == 0,
        codes[:, : cap // 2, None],
        jnp.where(lane == 1, codes[:, cap // 2 :, None], 0.0),
    )
    packed = jnp.concatenate(
        [rec_load[0, :, : cap // 2], rec_load[0, :, cap // 2 :], tags], axis=-1
    )
    arrived = lax.all_to_all(packed, "tm", split_axis=0, concat_axis=0)

    cube = 2 * modes * modes * modes
    probe_row = probe[None, :]
    (whole,) = call(compose_kernel, "compose", [mat], pos, retain, coupling, flops=21 * cube)
    other = lax.ppermute(whole, "tm", swap)
    both, chip = call(pair_kernel, "pair_map", [(2,) + mat, mat], pos, whole, other, flops=3 * cube)
    got = [lax.ppermute(chip, "tm", along_y(s)) for s in SHIFTS]
    y_maps, y_before, line = call(
        line_map_kernel,
        "line_map",
        [(NY,) + mat, (NY - 1,) + mat, mat],
        pos,
        chip,
        *got,
        flops=9 * cube,
    )
    got = [lax.ppermute(line, "tm", along_x(s)) for s in SHIFTS]
    x_maps, through, group = call(
        group_map_kernel,
        "group_map",
        [(NX,) + mat, (NY,) + mat, mat],
        pos,
        line,
        *got,
        y_before,
        scratch=[vm(NX, *mat)],
        flops=18 * cube,
    )
    g1 = later(group, 1)
    g2 = later(group, 2)
    (h1,) = call(product_kernel, "two_groups", [mat], pos, g2, g1, flops=3 * cube)
    h1_far = later(h1, 2)
    (h2,) = call(product_kernel, "four_groups", [mat], pos, h1_far, h1, flops=3 * cube)

    (weights,) = call(
        weights_kernel, "weights", [(steps, modes)], pos, retain, coupling, probe_row, flops=cube
    )
    shifted, kept, sent, driven = call(
        drive_kernel,
        "drive",
        [mat, (half, modes), (half, modes), (steps, samples)],
        pos,
        arrived,
        retain,
        coupling,
        probe_row,
        flops=60 * cube,
    )
    back = lax.ppermute(sent, "tm", swap)
    small = (part, modes)
    first, *rows = call(
        pair_shift_kernel,
        "pair_shift",
        [(half, modes)] + [small] * 4,
        pos,
        kept,
        back,
        both,
        scratch=[vm(half, modes)],
        flops=cube,
    )
    got = [lax.ppermute(r, "tm", along_y(s)) for r, s in zip(rows[1:], SHIFTS)]
    b_before, b_line = call(
        line_shift_kernel,
        "line_shift",
        [(NY - 1,) + small, small],
        pos,
        rows[0],
        *got,
        y_maps,
        scratch=[vm(NY, *small)],
        flops=cube,
    )
    got = [lax.ppermute(b_line, "tm", along_x(s)) for s in SHIFTS]
    b_through, b_group = call(
        group_shift_kernel,
        "group_shift",
        [(NY,) + small, small],
        pos,
        b_line,
        *got,
        x_maps,
        y_before,
        b_before,
        scratch=[vm(NX, *small), vm(NX, *small)],
        flops=2 * cube,
    )
    (e,) = call(
        first_hop_kernel,
        "hop1",
        [small],
        pos,
        initial_state,
        later(b_group, 1),
        later(b_group, 2),
        g1,
        flops=cube,
    )
    (e,) = call(hop_kernel, "hop2", [small], pos, e, later(e, 2), h1, flops=cube)
    rows = call(
        last_hop_kernel,
        "hop4",
        [small] * 4,
        pos,
        e,
        later(e, 4),
        h2,
        through,
        b_through,
        scratch=[vm(NY, *small)],
        flops=2 * cube,
    )
    got = [lax.ppermute(r, "tm", along_y(s)) for r, s in zip(rows[1:], SHIFTS)]
    kept, sent = call(
        chip_kernel,
        "chip_start",
        [(half, modes)] * 2,
        pos,
        rows[0],
        *got,
        both,
        first,
        scratch=[vm(half, modes)],
        flops=cube,
    )
    back = lax.ppermute(sent, "tm", swap)
    observed, final = call(
        finish_kernel,
        "finish",
        [(steps, samples), mat],
        pos,
        kept,
        back,
        whole,
        shifted,
        weights,
        driven,
        scratch=[vm(samples, modes)],
        flops=3 * cube,
    )
    return observed, final[None]


def solution(mesh):
    in_specs = (
        P(),
        P(("grp", "tm"), None),
        P(("grp", "tm"), None, None),
        P(),
        P(("grp", "tm"), None, None),
        P(("grp", "tm"), None, None),
        P(("grp", "tm"), None),
        P(("grp", "tm"), None, None, None),
    )
    out_specs = (P(("grp", "tm"), None), P(("grp", "tm"), None, None))
    return jax.shard_map(body, mesh=mesh, in_specs=in_specs, out_specs=out_specs, check_vma=False)
```

```python
import functools

import jax
import jax.numpy as jnp
from jax import lax
from jax.experimental import pallas as pl
from jax.experimental.pallas import tpu as pltpu
from jax.sharding import PartitionSpec as P

F32 = jnp.float32
BF16 = jnp.bfloat16
NY = 4
NX = 4
SHIFTS = (1, 3, 2)


def split(a):
    hi = a.astype(BF16)
    return hi, (a - hi.astype(F32)).astype(BF16)


def dot(a, b, transposed=False):
    dims = (((1,), (1 if transposed else 0,)), ((), ()))
    return lax.dot_general(a, b, dims, preferred_element_type=F32)


def mm(left, right, transposed=False):
    ah, al = left
    bh, bl = right
    return dot(ah, bh, transposed) + (dot(ah, bl, transposed) + dot(al, bh, transposed))


def call(kernel, name, outs, *args, scratch=(), flops=0, after=()):
    shapes = [s if hasattr(s, "dtype") else jax.ShapeDtypeStruct(s, F32) for s in outs]
    smem = pl.BlockSpec(memory_space=pltpu.SMEM)
    vmem = pl.BlockSpec(memory_space=pltpu.VMEM)
    moved = sum(4 * a.size for a in args) + sum(4 * s.size for s in shapes)
    n_args, n_after = len(args), len(after)

    def run(*refs):
        kernel(*refs[:n_args], *refs[n_args + n_after :])

    return pl.pallas_call(
        run,
        out_shape=shapes,
        in_specs=[smem] + [vmem] * (n_args - 1) + [pl.BlockSpec(memory_space=pl.ANY)] * n_after,
        out_specs=[vmem] * len(shapes),
        scratch_shapes=list(scratch),
        name=name,
        cost_estimate=pl.CostEstimate(flops=flops, bytes_accessed=moved, transcendentals=0),
        compiler_params=pltpu.CompilerParams(vmem_limit_bytes=16 * 1024 * 1024),
    )(*args, *after)


def pack_kernel(loads, samples_of, steps_of, counts, *refs, samples):
    out, samples_buf, steps_buf, counts_buf, tags, sems = refs[-6:]
    owners, cap, modes = loads.shape
    half = cap // 2
    copies = [
        pltpu.make_async_copy(samples_of, samples_buf, sems.at[0]),
        pltpu.make_async_copy(steps_of, steps_buf, sems.at[1]),
        pltpu.make_async_copy(counts, counts_buf, sems.at[2]),
        pltpu.make_async_copy(loads.at[:, :half, :], out.at[:, :, 0:modes], sems.at[3]),
        pltpu.make_async_copy(loads.at[:, half:, :], out.at[:, :, modes : 2 * modes], sems.at[4]),
    ]
    for copy in copies:
        copy.start()
    for copy in copies[:3]:
        copy.wait()
    slot = lax.broadcasted_iota(jnp.int32, (cap, owners), 0)
    codes = jnp.where(slot < counts_buf[...], steps_buf[...] * samples + samples_buf[...], -1)
    codes = codes.astype(F32)
    lane = lax.broadcasted_iota(jnp.int32, (half, 128), 1)
    for j in range(owners):
        tags[j] = jnp.where(lane == 0, codes[:half, j : j + 1], codes[half:, j : j + 1])
    last = pltpu.make_async_copy(tags, out.at[:, :, 2 * modes : 2 * modes + 128], sems.at[5])
    last.start()
    for copy in copies[3:]:
        copy.wait()
    last.wait()


def compose_kernel(pos, retain, coupling, probe, whole, seen):
    steps, modes = retain.shape
    rows = lax.broadcasted_iota(jnp.int32, (modes, modes), 0)
    cols = lax.broadcasted_iota(jnp.int32, (modes, modes), 1)
    total = coupling[0].T + jnp.where(rows == cols, retain[0:1, :], 0.0)
    step = lax.broadcasted_iota(jnp.int32, (steps, modes), 0)
    state = jnp.zeros((steps, modes), F32)
    for t in range(steps):
        u = steps - 1 - t
        state = jnp.where(step == u, probe[...], state)
        state = state * retain[u : u + 1, :] + mm(split(state), split(coupling[u]))
        if t > 0:
            total = total * retain[t : t + 1, :] + mm(split(total), split(coupling[t]), True)
    whole[...] = total
    seen[...] = state


def drive_kernel(pos, arrived, retain, coupling, probe, shifted, kept, sent, seen):
    steps, modes = retain.shape
    sources, half, _ = arrived.shape
    n = sources * half
    samples = shifted.shape[0]
    loads = jnp.concatenate(
        [
            arrived[:, :, 0:modes].reshape(n, modes),
            arrived[:, :, modes : 2 * modes].reshape(n, modes),
        ],
        axis=0,
    )
    lh, ll = split(loads)
    codes = arrived[:, :, 2 * modes : 2 * modes + 128].reshape(n, 128).T
    codes = jnp.concatenate([codes[0:1, :], codes[1:2, :]], axis=1).astype(jnp.int32)
    place = lax.broadcasted_iota(jnp.int32, (samples, 2 * n), 0)
    lane = lax.broadcasted_iota(jnp.int32, (samples, 128), 1)
    shown = jnp.zeros((samples, 128), F32)
    field = None
    for t in range(steps):
        hit = jnp.where(place + t * samples == codes, 1.0, 0.0).astype(BF16)
        kick = dot(hit, lh) + dot(hit, ll)
        if t > 0:
            kick = kick + field * retain[t : t + 1, :] + mm(parts, split(coupling[t]), True)
        field = kick
        parts = split(field)
        shown = jnp.where(lane == t, jnp.sum(field * probe[...], axis=1, keepdims=True), shown)
    shifted[...] = field
    seen[...] = shown.T[:steps]
    c = pos[0]
    h = samples // 2

    @pl.when(c == 0)
    def _():
        kept[...] = field[:h]
        sent[...] = field[h:]

    @pl.when(c != 0)
    def _():
        kept[...] = field[h:]
        sent[...] = field[:h]


def pair_kernel(pos, mine, other, both, chip):
    c = pos[0]

    @pl.when(c == 0)
    def _():
        both[0] = mine[...]
        both[1] = other[...]

    @pl.when(c != 0)
    def _():
        both[0] = other[...]
        both[1] = mine[...]

    chip[...] = mm(split(both[0]), split(both[1]))


def order(place, count, ordered, refs):
    ordered[place] = refs[0][...]
    for s, ref in zip(SHIFTS, refs[1:]):
        ordered[lax.rem(place + count - s, count)] = ref[...]


def line_map_kernel(pos, a0, a1, a3, a2, ordered, prefix, line):
    order(pos[1], NY, ordered, (a0, a1, a3, a2))
    total = ordered[0]
    for k in range(1, NY):
        prefix[k - 1] = total
        total = mm(split(total), split(ordered[k]))
    line[...] = total


def group_map_kernel(pos, a0, a1, a3, a2, prefix, ordered, through, high, low, before):
    x = pos[2]
    order(x, NX, ordered, (a0, a1, a3, a2))
    modes = high.shape[0]
    rows = lax.broadcasted_iota(jnp.int32, (modes, modes), 0)
    cols = lax.broadcasted_iota(jnp.int32, (modes, modes), 1)
    before[0] = jnp.where(rows == cols, 1.0, 0.0)
    total = ordered[0]
    for k in range(1, NX):
        before[k] = total
        total = mm(split(total), split(ordered[k]))
    high[...], low[...] = split(total)
    own = before[x]
    through[0] = own
    own = split(own)
    for k in range(1, NY):
        through[k] = mm(own, split(prefix[k - 1]))


def pair_shift_kernel(pos, kept, got, both, first, s0, s1, s3, s2, chip):
    c = pos[0]
    y = pos[1]
    r = s0.shape[0]
    mine = kept[...]
    theirs = got[...]
    zero = jnp.where(c == 0, mine, theirs)
    one = jnp.where(c == 0, theirs, mine)
    first[...] = zero
    chip[...] = mm(split(zero), split(both[1])) + one
    for s, out in zip((0,) + SHIFTS, (s0, s1, s3, s2)):
        start = pl.multiple_of(lax.rem(y + s, NY) * r, r)
        out[...] = chip[pl.ds(start, r), :]


def line_shift_kernel(pos, b0, b1, b3, b2, maps, before, line, ordered):
    order(pos[1], NY, ordered, (b0, b1, b3, b2))
    total = ordered[0]
    for k in range(1, NY):
        before[k - 1] = total
        total = mm(split(total), split(maps[k])) + ordered[k]
    line[...] = total


def group_shift_kernel(pos, b0, b1, b3, b2, maps, prefix, before, through, group, ordered, own):
    x = pos[2]
    order(x, NX, ordered, (b0, b1, b3, b2))
    own[0] = jnp.zeros_like(ordered[0])
    total = ordered[0]
    for k in range(1, NX):
        own[k] = total
        total = mm(split(total), split(maps[k])) + ordered[k]
    group[...] = total
    prior = own[x]
    through[0] = prior
    prior = split(prior)
    for k in range(1, NY):
        through[k] = mm(prior, split(prefix[k - 1])) + before[k - 1]


def released_rows(pos, initial, part):
    start = pl.multiple_of(pos[0] * (NY * part) + pos[1] * part, part)
    return initial[pl.ds(start, part), :]


def first_hop_kernel(pos, initial, high, low, shift, out):
    state = released_rows(pos, initial, out.shape[0])
    out[...] = mm(split(state), (high[...], low[...])) + shift[...]


def hop_kernel(pos, got, high, low, shift, out):
    out[...] = mm(split(got[...]), (high[...], low[...])) + shift[...]


def last_hop_kernel(pos, initial, *refs):
    gots, (maps, shifts, s0, s1, s3, s2, chips) = refs[:-7], refs[-7:]
    y = pos[1]
    g = pos[3]
    state = released_rows(pos, initial, s0.shape[0])
    for k, got in enumerate(gots):
        state = jnp.where(g == k + 1, got[...], state)
    group = split(state)
    for k in range(NY):
        chips[k] = mm(group, split(maps[k])) + shifts[k]
    for s, out in zip((0,) + SHIFTS, (s0, s1, s3, s2)):
        out[...] = chips[lax.rem(y + s, NY)]


def chip_kernel(pos, e0, e1, e3, e2, both, first, kept, sent, chip):
    c, y = pos[0], pos[1]
    r = e0.shape[0]
    for s, ref in zip((0,) + SHIFTS, (e0, e1, e3, e2)):
        start = pl.multiple_of(lax.rem(y + NY - s, NY) * r, r)
        chip[pl.ds(start, r), :] = ref[...]
    zero = chip[...]
    one = mm(split(zero), split(both[0])) + first[...]
    kept[...] = jnp.where(c == 0, zero, one)
    sent[...] = jnp.where(c == 0, one, zero)


def finish_kernel(pos, kept, got, whole, shifted, weights, driven, observed, final, start):
    c = pos[0]
    h = kept.shape[0]

    @pl.when(c == 0)
    def _():
        start[:h] = kept[...]
        start[h:] = got[...]

    @pl.when(c != 0)
    def _():
        start[:h] = got[...]
        start[h:] = kept[...]

    parts = split(start[...])
    final[...] = mm(parts, split(whole[...])) + shifted[...]
    observed[...] = mm(split(weights[...]), parts, True) + driven[...]


def body(initial_state, retain, coupling, probe, rec_sample, rec_step, rec_count, rec_load):
    steps, modes, _ = coupling.shape
    samples = initial_state.shape[0]
    owners, cap = rec_sample.shape[1:]
    half = samples // 2
    part = half // NY
    mat = (modes, modes)
    vm = lambda *s: pltpu.VMEM(s, F32)

    t = lax.axis_index("tm")
    g = lax.axis_index("grp")
    pos = jnp.stack([t % 2, (t // 2) % NY, t // (2 * NY), g]).astype(jnp.int32)

    def at(x, y, c):
        return (x * NY + y) * 2 + c

    spots = [(x, y, c) for x in range(NX) for y in range(NY) for c in range(2)]
    swap = [(at(x, y, c), at(x, y, 1 - c)) for x, y, c in spots]

    def along_y(s):
        return [(at(x, y, c), at(x, (y + s) % NY, c)) for x, y, c in spots]

    def along_x(s):
        return [(at(x, y, c), at((x + s) % NX, y, c)) for x, y, c in spots]

    n_grp = lax.axis_size("grp")

    cube = 2 * modes * modes * modes
    probe_row = probe[None, :]
    whole, weights = call(
        compose_kernel,
        "compose",
        [mat, (steps, modes)],
        pos,
        retain,
        coupling,
        probe_row,
        flops=22 * cube,
    )
    other = lax.ppermute(whole, "tm", swap)
    both, chip = call(pair_kernel, "pair_map", [(2,) + mat, mat], pos, whole, other, flops=3 * cube)
    got = [lax.ppermute(chip, "tm", along_y(s)) for s in SHIFTS]
    anywhere = pl.BlockSpec(memory_space=pl.ANY)
    shape = (owners, cap // 2, 2 * modes + 128)
    packed = pl.pallas_call(
        functools.partial(pack_kernel, samples=samples),
        out_shape=jax.ShapeDtypeStruct(shape, F32),
        in_specs=[anywhere] * 5,
        out_specs=anywhere,
        scratch_shapes=[
            pltpu.VMEM((cap, owners), jnp.int32),
            pltpu.VMEM((cap, owners), jnp.int32),
            pltpu.VMEM((1, owners), jnp.int32),
            vm(owners, cap // 2, 128),
            pltpu.SemaphoreType.DMA((6,)),
        ],
        name="pack",
        cost_estimate=pl.CostEstimate(flops=0, bytes_accessed=2**20, transcendentals=0),
    )(rec_load[0], rec_sample[0].T, rec_step[0].T, rec_count, chip)
    arrived = lax.all_to_all(packed, "tm", split_axis=0, concat_axis=0)
    y_maps, y_before, line = call(
        line_map_kernel,
        "line_map",
        [(NY,) + mat, (NY - 1,) + mat, mat],
        pos,
        chip,
        *got,
        flops=9 * cube,
        after=(packed,),
    )
    got = [lax.ppermute(line, "tm", along_x(s)) for s in SHIFTS]
    shifted, kept, sent, driven = call(
        drive_kernel,
        "drive",
        [mat, (half, modes), (half, modes), (steps, samples)],
        pos,
        arrived,
        retain,
        coupling,
        probe_row,
        flops=60 * cube,
        after=(line,),
    )
    half_mat = jax.ShapeDtypeStruct(mat, BF16)
    x_maps, through, high, low = call(
        group_map_kernel,
        "group_map",
        [(NX,) + mat, (NY,) + mat, half_mat, half_mat],
        pos,
        line,
        *got,
        y_before,
        scratch=[vm(NX, *mat)],
        flops=18 * cube,
    )
    back = lax.ppermute(sent, "tm", swap)
    small = (part, modes)
    first, *rows = call(
        pair_shift_kernel,
        "pair_shift",
        [(half, modes)] + [small] * 4,
        pos,
        kept,
        back,
        both,
        scratch=[vm(half, modes)],
        flops=cube,
    )
    got = [lax.ppermute(r, "tm", along_y(s)) for r, s in zip(rows[1:], SHIFTS)]
    b_before, b_line = call(
        line_shift_kernel,
        "line_shift",
        [(NY - 1,) + small, small],
        pos,
        rows[0],
        *got,
        y_maps,
        scratch=[vm(NY, *small)],
        flops=cube,
    )
    got = [lax.ppermute(b_line, "tm", along_x(s)) for s in SHIFTS]
    b_through, b_group = call(
        group_shift_kernel,
        "group_shift",
        [(NY,) + small, small],
        pos,
        b_line,
        *got,
        x_maps,
        y_before,
        b_before,
        scratch=[vm(NX, *small), vm(NX, *small)],
        flops=2 * cube,
    )
    (e,) = call(
        first_hop_kernel, "hop0", [small], pos, initial_state, high, low, b_group, flops=cube
    )
    carried = [lax.ppermute(e, "grp", [(0, 1)])]
    for k in range(1, n_grp - 1):
        (e,) = call(hop_kernel, "hop", [small], pos, carried[-1], high, low, b_group, flops=cube)
        carried.append(lax.ppermute(e, "grp", [(k, k + 1)]))
    rows = call(
        last_hop_kernel,
        "chips",
        [small] * 4,
        pos,
        initial_state,
        *carried,
        through,
        b_through,
        scratch=[vm(NY, *small)],
        flops=2 * cube,
    )
    got = [lax.ppermute(r, "tm", along_y(s)) for r, s in zip(rows[1:], SHIFTS)]
    kept, sent = call(
        chip_kernel,
        "chip_start",
        [(half, modes)] * 2,
        pos,
        rows[0],
        *got,
        both,
        first,
        scratch=[vm(half, modes)],
        flops=cube,
    )
    back = lax.ppermute(sent, "tm", swap)
    observed, final = call(
        finish_kernel,
        "finish",
        [(steps, samples), mat],
        pos,
        kept,
        back,
        whole,
        shifted,
        weights,
        driven,
        scratch=[vm(samples, modes)],
        flops=3 * cube,
    )
    return observed, final[None]


def solution(mesh):
    in_specs = (
        P(),
        P(("grp", "tm"), None),
        P(("grp", "tm"), None, None),
        P(),
        P(("grp", "tm"), None, None),
        P(("grp", "tm"), None, None),
        P(("grp", "tm"), None),
        P(("grp", "tm"), None, None, None),
    )
    out_specs = (P(("grp", "tm"), None), P(("grp", "tm"), None, None))
    return jax.shard_map(body, mesh=mesh, in_specs=in_specs, out_specs=out_specs, check_vma=False)
```

```python
import functools

import jax
import jax.numpy as jnp
from jax import lax
from jax.experimental import pallas as pl
from jax.experimental.pallas import tpu as pltpu
from jax.sharding import PartitionSpec as P

F32 = jnp.float32
BF16 = jnp.bfloat16
NY = 4
NX = 4
SHIFTS = (1, 3, 2)


def split(a):
    hi = a.astype(BF16)
    return hi, (a - hi.astype(F32)).astype(BF16)


def dot(a, b, transposed=False):
    dims = (((1,), (1 if transposed else 0,)), ((), ()))
    return lax.dot_general(a, b, dims, preferred_element_type=F32)


def mm(left, right, transposed=False):
    ah, al = left
    bh, bl = right
    return dot(ah, bh, transposed) + (dot(ah, bl, transposed) + dot(al, bh, transposed))


def call(kernel, name, outs, *args, scratch=(), flops=0, after=()):
    shapes = [s if hasattr(s, "dtype") else jax.ShapeDtypeStruct(s, F32) for s in outs]
    smem = pl.BlockSpec(memory_space=pltpu.SMEM)
    vmem = pl.BlockSpec(memory_space=pltpu.VMEM)
    moved = sum(4 * a.size for a in args) + sum(4 * s.size for s in shapes)
    n_args, n_after = len(args), len(after)

    def run(*refs):
        kernel(*refs[:n_args], *refs[n_args + n_after :])

    return pl.pallas_call(
        run,
        out_shape=shapes,
        in_specs=[smem] + [vmem] * (n_args - 1) + [pl.BlockSpec(memory_space=pl.ANY)] * n_after,
        out_specs=[vmem] * len(shapes),
        scratch_shapes=list(scratch),
        name=name,
        cost_estimate=pl.CostEstimate(flops=flops, bytes_accessed=moved, transcendentals=0),
        compiler_params=pltpu.CompilerParams(vmem_limit_bytes=16 * 1024 * 1024),
    )(*args, *after)


def pack_kernel(loads, samples_of, steps_of, counts, out, samples_buf, steps_buf, counts_buf, sems, *, samples):
    owners, cap, modes = loads.shape
    half = cap // 2
    copies = [
        pltpu.make_async_copy(samples_of, samples_buf, sems.at[0]),
        pltpu.make_async_copy(steps_of, steps_buf, sems.at[1]),
        pltpu.make_async_copy(counts, counts_buf, sems.at[2]),
        pltpu.make_async_copy(loads.at[:, :half, :], out.at[:, :, 0:modes], sems.at[3]),
        pltpu.make_async_copy(loads.at[:, half:, :], out.at[:, :, modes : 2 * modes], sems.at[4]),
    ]
    for copy in copies:
        copy.start()
    for copy in copies[:3]:
        copy.wait()
    slot = lax.broadcasted_iota(jnp.int32, (cap, owners), 0)
    codes = jnp.where(slot < counts_buf[...], steps_buf[...] * samples + samples_buf[...], -1)
    codes = codes.astype(F32)
    lane = lax.broadcasted_iota(jnp.int32, (half, 128), 1)
    for j in range(owners):
        out[j, :, 2 * modes :] = jnp.where(
            lane == 0, codes[:half, j : j + 1], codes[half:, j : j + 1]
        )
    for copy in copies[3:]:
        copy.wait()


def compose_kernel(pos, retain, coupling, probe, whole, seen):
    steps, modes = retain.shape
    rows = lax.broadcasted_iota(jnp.int32, (modes, modes), 0)
    cols = lax.broadcasted_iota(jnp.int32, (modes, modes), 1)
    total = coupling[0].T + jnp.where(rows == cols, retain[0:1, :], 0.0)
    step = lax.broadcasted_iota(jnp.int32, (steps, modes), 0)
    state = jnp.zeros((steps, modes), F32)
    for t in range(steps):
        u = steps - 1 - t
        state = jnp.where(step == u, probe[...], state)
        state = state * retain[u : u + 1, :] + mm(split(state), split(coupling[u]))
        if t > 0:
            total = total * retain[t : t + 1, :] + mm(split(total), split(coupling[t]), True)
    whole[...] = total
    seen[...] = state


def drive_kernel(pos, arrived, retain, coupling, probe, shifted, kept, sent, seen):
    steps, modes = retain.shape
    sources, half, _ = arrived.shape
    n = sources * half
    samples = shifted.shape[0]
    loads = jnp.concatenate(
        [
            arrived[:, :, 0:modes].reshape(n, modes),
            arrived[:, :, modes : 2 * modes].reshape(n, modes),
        ],
        axis=0,
    )
    lh, ll = split(loads)
    codes = arrived[:, :, 2 * modes : 2 * modes + 128].reshape(n, 128).T
    codes = jnp.concatenate([codes[0:1, :], codes[1:2, :]], axis=1).astype(jnp.int32)
    place = lax.broadcasted_iota(jnp.int32, (samples, 2 * n), 0)
    lane = lax.broadcasted_iota(jnp.int32, (samples, 128), 1)
    shown = jnp.zeros((samples, 128), F32)
    field = None
    for t in range(steps):
        hit = jnp.where(place + t * samples == codes, 1.0, 0.0).astype(BF16)
        kick = dot(hit, lh) + dot(hit, ll)
        if t > 0:
            kick = kick + field * retain[t : t + 1, :] + mm(parts, split(coupling[t]), True)
        field = kick
        parts = split(field)
        shown = jnp.where(lane == t, jnp.sum(field * probe[...], axis=1, keepdims=True), shown)
    shifted[...] = field
    seen[...] = shown.T[:steps]
    c = pos[0]
    h = samples // 2

    @pl.when(c == 0)
    def _():
        kept[...] = field[:h]
        sent[...] = field[h:]

    @pl.when(c != 0)
    def _():
        kept[...] = field[h:]
        sent[...] = field[:h]


def pair_kernel(pos, mine, other, both, chip):
    c = pos[0]

    @pl.when(c == 0)
    def _():
        both[0] = mine[...]
        both[1] = other[...]

    @pl.when(c != 0)
    def _():
        both[0] = other[...]
        both[1] = mine[...]

    chip[...] = mm(split(both[0]), split(both[1]))


def order(place, count, ordered, refs):
    ordered[place] = refs[0][...]
    for s, ref in zip(SHIFTS, refs[1:]):
        ordered[lax.rem(place + count - s, count)] = ref[...]


def line_map_kernel(pos, a0, a1, a3, a2, ordered, prefix, line):
    order(pos[1], NY, ordered, (a0, a1, a3, a2))
    total = ordered[0]
    for k in range(1, NY):
        prefix[k - 1] = total
        total = mm(split(total), split(ordered[k]))
    line[...] = total


def group_map_kernel(pos, a0, a1, a3, a2, prefix, ordered, through, high, low, before):
    x = pos[2]
    order(x, NX, ordered, (a0, a1, a3, a2))
    modes = high.shape[0]
    rows = lax.broadcasted_iota(jnp.int32, (modes, modes), 0)
    cols = lax.broadcasted_iota(jnp.int32, (modes, modes), 1)
    before[0] = jnp.where(rows == cols, 1.0, 0.0)
    total = ordered[0]
    for k in range(1, NX):
        before[k] = total
        total = mm(split(total), split(ordered[k]))
    high[...], low[...] = split(total)
    own = before[x]
    through[0] = own
    own = split(own)
    for k in range(1, NY):
        through[k] = mm(own, split(prefix[k - 1]))


def pair_shift_kernel(pos, kept, got, both, first, s0, s1, s3, s2, chip):
    c = pos[0]
    y = pos[1]
    r = s0.shape[0]
    mine = kept[...]
    theirs = got[...]
    zero = jnp.where(c == 0, mine, theirs)
    one = jnp.where(c == 0, theirs, mine)
    first[...] = zero
    chip[...] = mm(split(zero), split(both[1])) + one
    for s, out in zip((0,) + SHIFTS, (s0, s1, s3, s2)):
        start = pl.multiple_of(lax.rem(y + s, NY) * r, r)
        out[...] = chip[pl.ds(start, r), :]


def line_shift_kernel(pos, b0, b1, b3, b2, maps, before, line, ordered):
    order(pos[1], NY, ordered, (b0, b1, b3, b2))
    total = ordered[0]
    for k in range(1, NY):
        before[k - 1] = total
        total = mm(split(total), split(maps[k])) + ordered[k]
    line[...] = total


def group_shift_kernel(pos, b0, b1, b3, b2, maps, prefix, before, through, group, ordered, own):
    x = pos[2]
    order(x, NX, ordered, (b0, b1, b3, b2))
    own[0] = jnp.zeros_like(ordered[0])
    total = ordered[0]
    for k in range(1, NX):
        own[k] = total
        total = mm(split(total), split(maps[k])) + ordered[k]
    group[...] = total
    prior = own[x]
    through[0] = prior
    prior = split(prior)
    for k in range(1, NY):
        through[k] = mm(prior, split(prefix[k - 1])) + before[k - 1]


def released_rows(pos, initial, part):
    start = pl.multiple_of(pos[0] * (NY * part) + pos[1] * part, part)
    return initial[pl.ds(start, part), :]


def first_hop_kernel(pos, initial, high, low, shift, out):
    state = released_rows(pos, initial, out.shape[0])
    out[...] = mm(split(state), (high[...], low[...])) + shift[...]


def hop_kernel(pos, got, high, low, shift, out):
    out[...] = mm(split(got[...]), (high[...], low[...])) + shift[...]


def last_hop_kernel(pos, initial, *refs):
    gots, (maps, shifts, s0, s1, s3, s2, chips) = refs[:-7], refs[-7:]
    y = pos[1]
    g = pos[3]
    state = released_rows(pos, initial, s0.shape[0])
    for k, got in enumerate(gots):
        state = jnp.where(g == k + 1, got[...], state)
    group = split(state)
    for k in range(NY):
        chips[k] = mm(group, split(maps[k])) + shifts[k]
    for s, out in zip((0,) + SHIFTS, (s0, s1, s3, s2)):
        out[...] = chips[lax.rem(y + s, NY)]


def chip_kernel(pos, e0, e1, e3, e2, both, first, kept, sent, chip):
    c, y = pos[0], pos[1]
    r = e0.shape[0]
    for s, ref in zip((0,) + SHIFTS, (e0, e1, e3, e2)):
        start = pl.multiple_of(lax.rem(y + NY - s, NY) * r, r)
        chip[pl.ds(start, r), :] = ref[...]
    zero = chip[...]
    one = mm(split(zero), split(both[0])) + first[...]
    kept[...] = jnp.where(c == 0, zero, one)
    sent[...] = jnp.where(c == 0, one, zero)


def finish_kernel(pos, kept, got, whole, shifted, weights, driven, observed, final, start):
    c = pos[0]
    h = kept.shape[0]

    @pl.when(c == 0)
    def _():
        start[:h] = kept[...]
        start[h:] = got[...]

    @pl.when(c != 0)
    def _():
        start[:h] = got[...]
        start[h:] = kept[...]

    parts = split(start[...])
    final[...] = mm(parts, split(whole[...])) + shifted[...]
    observed[...] = mm(split(weights[...]), parts, True) + driven[...]


def body(initial_state, retain, coupling, probe, rec_sample, rec_step, rec_count, rec_load):
    steps, modes, _ = coupling.shape
    samples = initial_state.shape[0]
    owners, cap = rec_sample.shape[1:]
    half = samples // 2
    part = half // NY
    mat = (modes, modes)
    vm = lambda *s: pltpu.VMEM(s, F32)

    t = lax.axis_index("tm")
    g = lax.axis_index("grp")
    pos = jnp.stack([t % 2, (t // 2) % NY, t // (2 * NY), g]).astype(jnp.int32)

    def at(x, y, c):
        return (x * NY + y) * 2 + c

    spots = [(x, y, c) for x in range(NX) for y in range(NY) for c in range(2)]
    swap = [(at(x, y, c), at(x, y, 1 - c)) for x, y, c in spots]

    def along_y(s):
        return [(at(x, y, c), at(x, (y + s) % NY, c)) for x, y, c in spots]

    def along_x(s):
        return [(at(x, y, c), at((x + s) % NX, y, c)) for x, y, c in spots]

    n_grp = lax.axis_size("grp")

    packed = pl.pallas_call(
        functools.partial(pack_kernel, samples=samples),
        out_shape=jax.ShapeDtypeStruct((owners, cap // 2, 2 * modes + 128), F32),
        in_specs=[pl.BlockSpec(memory_space=pltpu.HBM)] * 4,
        out_specs=pl.BlockSpec(memory_space=pltpu.VMEM),
        scratch_shapes=[
            pltpu.VMEM((cap, owners), jnp.int32),
            pltpu.VMEM((cap, owners), jnp.int32),
            pltpu.VMEM((1, owners), jnp.int32),
            pltpu.SemaphoreType.DMA((5,)),
        ],
        name="pack",
        cost_estimate=pl.CostEstimate(flops=0, bytes_accessed=2**20, transcendentals=0),
    )(rec_load[0], rec_sample[0].T, rec_step[0].T, rec_count)
    arrived = lax.all_to_all(packed, "tm", split_axis=0, concat_axis=0)

    cube = 2 * modes * modes * modes
    probe_row = probe[None, :]
    whole, weights = call(
        compose_kernel,
        "compose",
        [mat, (steps, modes)],
        pos,
        retain,
        coupling,
        probe_row,
        flops=22 * cube,
        after=(packed,),
    )
    other = lax.ppermute(whole, "tm", swap)
    both, chip = call(pair_kernel, "pair_map", [(2,) + mat, mat], pos, whole, other, flops=3 * cube)
    chips = [lax.ppermute(chip, "tm", along_y(s)) for s in SHIFTS]
    shifted, kept, sent, driven = call(
        drive_kernel,
        "drive",
        [mat, (half, modes), (half, modes), (steps, samples)],
        pos,
        arrived,
        retain,
        coupling,
        probe_row,
        flops=60 * cube,
    )
    back = lax.ppermute(sent, "tm", swap)
    small = (part, modes)
    first, *rows = call(
        pair_shift_kernel,
        "pair_shift",
        [(half, modes)] + [small] * 4,
        pos,
        kept,
        back,
        both,
        scratch=[vm(half, modes)],
        flops=cube,
    )
    got = [lax.ppermute(r, "tm", along_y(s)) for r, s in zip(rows[1:], SHIFTS)]
    y_maps, y_before, line = call(
        line_map_kernel,
        "line_map",
        [(NY,) + mat, (NY - 1,) + mat, mat],
        pos,
        chip,
        *chips,
        flops=9 * cube,
        after=got,
    )
    lines = [lax.ppermute(line, "tm", along_x(s)) for s in SHIFTS]
    half_mat = jax.ShapeDtypeStruct(mat, BF16)
    x_maps, through, high, low = call(
        group_map_kernel,
        "group_map",
        [(NX,) + mat, (NY,) + mat, half_mat, half_mat],
        pos,
        line,
        *lines,
        y_before,
        scratch=[vm(NX, *mat)],
        flops=18 * cube,
    )
    b_before, b_line = call(
        line_shift_kernel,
        "line_shift",
        [(NY - 1,) + small, small],
        pos,
        rows[0],
        *got,
        y_maps,
        scratch=[vm(NY, *small)],
        flops=cube,
    )
    got = [lax.ppermute(b_line, "tm", along_x(s)) for s in SHIFTS]
    b_through, b_group = call(
        group_shift_kernel,
        "group_shift",
        [(NY,) + small, small],
        pos,
        b_line,
        *got,
        x_maps,
        y_before,
        b_before,
        scratch=[vm(NX, *small), vm(NX, *small)],
        flops=2 * cube,
    )
    (e,) = call(
        first_hop_kernel, "hop0", [small], pos, initial_state, high, low, b_group, flops=cube
    )
    carried = [lax.ppermute(e, "grp", [(0, 1)])]
    for k in range(1, n_grp - 1):
        (e,) = call(hop_kernel, "hop", [small], pos, carried[-1], high, low, b_group, flops=cube)
        carried.append(lax.ppermute(e, "grp", [(k, k + 1)]))
    rows = call(
        last_hop_kernel,
        "chips",
        [small] * 4,
        pos,
        initial_state,
        *carried,
        through,
        b_through,
        scratch=[vm(NY, *small)],
        flops=2 * cube,
    )
    got = [lax.ppermute(r, "tm", along_y(s)) for r, s in zip(rows[1:], SHIFTS)]
    kept, sent = call(
        chip_kernel,
        "chip_start",
        [(half, modes)] * 2,
        pos,
        rows[0],
        *got,
        both,
        first,
        scratch=[vm(half, modes)],
        flops=cube,
    )
    back = lax.ppermute(sent, "tm", swap)
    observed, final = call(
        finish_kernel,
        "finish",
        [(steps, samples), mat],
        pos,
        kept,
        back,
        whole,
        shifted,
        weights,
        driven,
        scratch=[vm(samples, modes)],
        flops=3 * cube,
    )
    return observed, final[None]


def solution(mesh):
    in_specs = (
        P(),
        P(("grp", "tm"), None),
        P(("grp", "tm"), None, None),
        P(),
        P(("grp", "tm"), None, None),
        P(("grp", "tm"), None, None),
        P(("grp", "tm"), None),
        P(("grp", "tm"), None, None, None),
    )
    out_specs = (P(("grp", "tm"), None), P(("grp", "tm"), None, None))
    return jax.shard_map(body, mesh=mesh, in_specs=in_specs, out_specs=out_specs, check_vma=False)
```

```python
import functools

import jax
import jax.numpy as jnp
from jax import lax
from jax.experimental import pallas as pl
from jax.experimental.pallas import tpu as pltpu
from jax.sharding import PartitionSpec as P

F32 = jnp.float32
BF16 = jnp.bfloat16
NY = 4
NX = 4
SHIFTS = (1, 3, 2)


def split(a):
    hi = a.astype(BF16)
    return hi, (a - hi.astype(F32)).astype(BF16)


def dot(a, b, transposed=False):
    dims = (((1,), (1 if transposed else 0,)), ((), ()))
    return lax.dot_general(a, b, dims, preferred_element_type=F32)


def mm(left, right, transposed=False):
    ah, al = left
    bh, bl = right
    return dot(ah, bh, transposed) + (dot(ah, bl, transposed) + dot(al, bh, transposed))


def call(kernel, name, outs, *args, scratch=(), flops=0, after=()):
    shapes = [s if hasattr(s, "dtype") else jax.ShapeDtypeStruct(s, F32) for s in outs]
    smem = pl.BlockSpec(memory_space=pltpu.SMEM)
    vmem = pl.BlockSpec(memory_space=pltpu.VMEM)
    moved = sum(4 * a.size for a in args) + sum(4 * s.size for s in shapes)
    n_args, n_after = len(args), len(after)

    def run(*refs):
        kernel(*refs[:n_args], *refs[n_args + n_after :])

    return pl.pallas_call(
        run,
        out_shape=shapes,
        in_specs=[smem] + [vmem] * (n_args - 1) + [pl.BlockSpec(memory_space=pl.ANY)] * n_after,
        out_specs=[vmem] * len(shapes),
        scratch_shapes=list(scratch),
        name=name,
        cost_estimate=pl.CostEstimate(flops=flops, bytes_accessed=moved, transcendentals=0),
        compiler_params=pltpu.CompilerParams(vmem_limit_bytes=16 * 1024 * 1024),
    )(*args, *after)


def pack_kernel(loads, samples_of, steps_of, counts, out, samples_buf, steps_buf, counts_buf, sems, *, samples):
    owners, cap, modes = loads.shape
    half = cap // 2
    copies = [
        pltpu.make_async_copy(samples_of, samples_buf, sems.at[0]),
        pltpu.make_async_copy(steps_of, steps_buf, sems.at[1]),
        pltpu.make_async_copy(counts, counts_buf, sems.at[2]),
        pltpu.make_async_copy(loads.at[:, :half, :], out.at[:, :, 0:modes], sems.at[3]),
        pltpu.make_async_copy(loads.at[:, half:, :], out.at[:, :, modes : 2 * modes], sems.at[4]),
    ]
    for copy in copies:
        copy.start()
    for copy in copies[:3]:
        copy.wait()
    slot = lax.broadcasted_iota(jnp.int32, (cap, owners), 0)
    codes = jnp.where(slot < counts_buf[...], steps_buf[...] * samples + samples_buf[...], -1)
    codes = codes.astype(F32)
    lane = lax.broadcasted_iota(jnp.int32, (half, 128), 1)
    for j in range(owners):
        out[j, :, 2 * modes :] = jnp.where(
            lane == 0, codes[:half, j : j + 1], codes[half:, j : j + 1]
        )
    for copy in copies[3:]:
        copy.wait()


def compose_kernel(pos, retain, coupling, probe, whole, seen):
    steps, modes = retain.shape
    rows = lax.broadcasted_iota(jnp.int32, (modes, modes), 0)
    cols = lax.broadcasted_iota(jnp.int32, (modes, modes), 1)
    total = coupling[0].T + jnp.where(rows == cols, retain[0:1, :], 0.0)
    step = lax.broadcasted_iota(jnp.int32, (steps, modes), 0)
    state = jnp.zeros((steps, modes), F32)
    for t in range(steps):
        u = steps - 1 - t
        state = jnp.where(step == u, probe[...], state)
        state = state * retain[u : u + 1, :] + mm(split(state), split(coupling[u]))
        if t > 0:
            total = total * retain[t : t + 1, :] + mm(split(total), split(coupling[t]), True)
    whole[...] = total
    seen[...] = state


def drive_kernel(pos, arrived, retain, coupling, probe, shifted, kept, sent, seen):
    steps, modes = retain.shape
    sources, half, _ = arrived.shape
    n = sources * half
    samples = shifted.shape[0]
    loads = jnp.concatenate(
        [
            arrived[:, :, 0:modes].reshape(n, modes),
            arrived[:, :, modes : 2 * modes].reshape(n, modes),
        ],
        axis=0,
    )
    lh, ll = split(loads)
    codes = arrived[:, :, 2 * modes : 2 * modes + 128].reshape(n, 128).T
    codes = jnp.concatenate([codes[0:1, :], codes[1:2, :]], axis=1).astype(jnp.int32)
    place = lax.broadcasted_iota(jnp.int32, (samples, 2 * n), 0)
    lane = lax.broadcasted_iota(jnp.int32, (samples, 128), 1)
    shown = jnp.zeros((samples, 128), F32)
    field = None
    for t in range(steps):
        hit = jnp.where(place + t * samples == codes, 1.0, 0.0).astype(BF16)
        kick = dot(hit, lh) + dot(hit, ll)
        if t > 0:
            kick = kick + field * retain[t : t + 1, :] + mm(parts, split(coupling[t]), True)
        field = kick
        parts = split(field)
        shown = jnp.where(lane == t, jnp.sum(field * probe[...], axis=1, keepdims=True), shown)
    shifted[...] = field
    seen[...] = shown.T[:steps]
    c = pos[0]
    h = samples // 2

    @pl.when(c == 0)
    def _():
        kept[...] = field[:h]
        sent[...] = field[h:]

    @pl.when(c != 0)
    def _():
        kept[...] = field[h:]
        sent[...] = field[:h]


def pair_kernel(pos, mine, other, both, chip):
    c = pos[0]

    @pl.when(c == 0)
    def _():
        both[0] = mine[...]
        both[1] = other[...]

    @pl.when(c != 0)
    def _():
        both[0] = other[...]
        both[1] = mine[...]

    chip[...] = mm(split(both[0]), split(both[1]))


def order(place, count, ordered, refs):
    ordered[place] = refs[0][...]
    for s, ref in zip(SHIFTS, refs[1:]):
        ordered[lax.rem(place + count - s, count)] = ref[...]


def line_map_kernel(pos, a0, a1, a3, a2, ordered, prefix, line):
    order(pos[1], NY, ordered, (a0, a1, a3, a2))
    total = ordered[0]
    for k in range(1, NY):
        prefix[k - 1] = total
        total = mm(split(total), split(ordered[k]))
    line[...] = total


def group_map_kernel(pos, a0, a1, a3, a2, prefix, ordered, through, high, low, before):
    y = pos[1]
    x = pos[2]
    order(x, NX, ordered, (a0, a1, a3, a2))
    modes = high.shape[0]
    rows = lax.broadcasted_iota(jnp.int32, (modes, modes), 0)
    cols = lax.broadcasted_iota(jnp.int32, (modes, modes), 1)
    before[0] = jnp.where(rows == cols, 1.0, 0.0)
    total = ordered[0]
    for k in range(1, NX):
        before[k] = total
        total = mm(split(total), split(ordered[k]))
    high[...], low[...] = split(total)
    through[...] = before[x]

    @pl.when(y > 0)
    def _():
        through[...] = mm(split(before[x]), split(prefix[jnp.maximum(y - 1, 0)]))


def pair_shift_kernel(pos, kept, got, both, first, s0, s1, s3, s2, chip):
    c = pos[0]
    y = pos[1]
    r = s0.shape[0]
    mine = kept[...]
    theirs = got[...]
    zero = jnp.where(c == 0, mine, theirs)
    one = jnp.where(c == 0, theirs, mine)
    first[...] = zero
    chip[...] = mm(split(zero), split(both[1])) + one
    for s, out in zip((0,) + SHIFTS, (s0, s1, s3, s2)):
        start = pl.multiple_of(lax.rem(y + s, NY) * r, r)
        out[...] = chip[pl.ds(start, r), :]


def line_shift_kernel(pos, b0, b1, b3, b2, maps, before, line, ordered):
    order(pos[1], NY, ordered, (b0, b1, b3, b2))
    total = ordered[0]
    for k in range(1, NY):
        before[k - 1] = total
        total = mm(split(total), split(maps[k])) + ordered[k]
    line[...] = total


def group_shift_kernel(
    pos, b0, b1, b3, b2, maps, prefix, before, s0, s1, s3, s2, group, ordered, own, chips
):
    x, y = pos[2], pos[1]
    order(x, NX, ordered, (b0, b1, b3, b2))
    own[0] = jnp.zeros_like(ordered[0])
    total = ordered[0]
    for k in range(1, NX):
        own[k] = total
        total = mm(split(total), split(maps[k])) + ordered[k]
    group[...] = total
    prior = own[x]
    chips[0] = prior
    prior = split(prior)
    for k in range(1, NY):
        chips[k] = mm(prior, split(prefix[k - 1])) + before[k - 1]
    for s, out in zip((0,) + SHIFTS, (s0, s1, s3, s2)):
        out[...] = chips[lax.rem(y + s, NY)]


def released_rows(pos, initial, part):
    start = pl.multiple_of(pos[0] * (NY * part) + pos[1] * part, part)
    return initial[pl.ds(start, part), :]


def first_hop_kernel(pos, initial, high, low, shift, out):
    state = released_rows(pos, initial, out.shape[0])
    out[...] = mm(split(state), (high[...], low[...])) + shift[...]


def hop_kernel(pos, got, high, low, shift, out):
    out[...] = mm(split(got[...]), (high[...], low[...])) + shift[...]


def last_hop_kernel(pos, got, high, low, shift, *refs):
    earlier, out = refs[:-1], refs[-1]
    g = pos[3]
    state = mm(split(got[...]), (high[...], low[...])) + shift[...]
    for k, ref in enumerate(earlier):
        state = jnp.where(g == k, ref[...], state)
    out[...] = state


def chip_kernel(
    pos, e0, e1, e3, e2, d0, d1, d3, d2, initial, through, both, first, kept, sent, state, driven
):
    c, y, g = pos[0], pos[1], pos[3]
    r = e0.shape[0]
    for s, ref, part in zip((0,) + SHIFTS, (e0, e1, e3, e2), (d0, d1, d3, d2)):
        start = pl.multiple_of(lax.rem(y + NY - s, NY) * r, r)
        state[pl.ds(start, r), :] = ref[...]
        driven[pl.ds(start, r), :] = part[...]
    h = kept.shape[0]
    released = initial[pl.ds(pl.multiple_of(c * h, h), h), :]
    group = jnp.where(g == 0, released, state[...])
    zero = mm(split(group), split(through[...])) + driven[...]
    one = mm(split(zero), split(both[0])) + first[...]
    kept[...] = jnp.where(c == 0, zero, one)
    sent[...] = jnp.where(c == 0, one, zero)


def finish_kernel(pos, kept, got, whole, shifted, weights, driven, observed, final, start):
    c = pos[0]
    h = kept.shape[0]

    @pl.when(c == 0)
    def _():
        start[:h] = kept[...]
        start[h:] = got[...]

    @pl.when(c != 0)
    def _():
        start[:h] = got[...]
        start[h:] = kept[...]

    parts = split(start[...])
    final[...] = mm(parts, split(whole[...])) + shifted[...]
    observed[...] = mm(split(weights[...]), parts, True) + driven[...]


def body(initial_state, retain, coupling, probe, rec_sample, rec_step, rec_count, rec_load):
    steps, modes, _ = coupling.shape
    samples = initial_state.shape[0]
    owners, cap = rec_sample.shape[1:]
    half = samples // 2
    part = half // NY
    mat = (modes, modes)
    vm = lambda *s: pltpu.VMEM(s, F32)

    t = lax.axis_index("tm")
    g = lax.axis_index("grp")
    pos = jnp.stack([t % 2, (t // 2) % NY, t // (2 * NY), g]).astype(jnp.int32)

    def at(x, y, c):
        return (x * NY + y) * 2 + c

    spots = [(x, y, c) for x in range(NX) for y in range(NY) for c in range(2)]
    swap = [(at(x, y, c), at(x, y, 1 - c)) for x, y, c in spots]

    def along_y(s):
        return [(at(x, y, c), at(x, (y + s) % NY, c)) for x, y, c in spots]

    def along_x(s):
        return [(at(x, y, c), at((x + s) % NX, y, c)) for x, y, c in spots]

    n_grp = lax.axis_size("grp")

    packed = pl.pallas_call(
        functools.partial(pack_kernel, samples=samples),
        out_shape=jax.ShapeDtypeStruct((owners, cap // 2, 2 * modes + 128), F32),
        in_specs=[pl.BlockSpec(memory_space=pltpu.HBM)] * 4,
        out_specs=pl.BlockSpec(memory_space=pltpu.VMEM),
        scratch_shapes=[
            pltpu.VMEM((cap, owners), jnp.int32),
            pltpu.VMEM((cap, owners), jnp.int32),
            pltpu.VMEM((1, owners), jnp.int32),
            pltpu.SemaphoreType.DMA((5,)),
        ],
        name="pack",
        cost_estimate=pl.CostEstimate(flops=0, bytes_accessed=2**20, transcendentals=0),
    )(rec_load[0], rec_sample[0].T, rec_step[0].T, rec_count)
    arrived = lax.all_to_all(packed, "tm", split_axis=0, concat_axis=0)

    cube = 2 * modes * modes * modes
    probe_row = probe[None, :]
    whole, weights = call(
        compose_kernel,
        "compose",
        [mat, (steps, modes)],
        pos,
        retain,
        coupling,
        probe_row,
        flops=22 * cube,
        after=(packed,),
    )
    other = lax.ppermute(whole, "tm", swap)
    both, chip = call(pair_kernel, "pair_map", [(2,) + mat, mat], pos, whole, other, flops=3 * cube)
    chips = [lax.ppermute(chip, "tm", along_y(s)) for s in SHIFTS]
    shifted, kept, sent, driven = call(
        drive_kernel,
        "drive",
        [mat, (half, modes), (half, modes), (steps, samples)],
        pos,
        arrived,
        retain,
        coupling,
        probe_row,
        flops=60 * cube,
    )
    back = lax.ppermute(sent, "tm", swap)
    small = (part, modes)
    first, *rows = call(
        pair_shift_kernel,
        "pair_shift",
        [(half, modes)] + [small] * 4,
        pos,
        kept,
        back,
        both,
        scratch=[vm(half, modes)],
        flops=cube,
    )
    got = [lax.ppermute(r, "tm", along_y(s)) for r, s in zip(rows[1:], SHIFTS)]
    y_maps, y_before, line = call(
        line_map_kernel,
        "line_map",
        [(NY,) + mat, (NY - 1,) + mat, mat],
        pos,
        chip,
        *chips,
        flops=9 * cube,
        after=got,
    )
    lines = [lax.ppermute(line, "tm", along_x(s)) for s in SHIFTS]
    half_mat = jax.ShapeDtypeStruct(mat, BF16)
    x_maps, through, high, low = call(
        group_map_kernel,
        "group_map",
        [(NX,) + mat, mat, half_mat, half_mat],
        pos,
        line,
        *lines,
        y_before,
        scratch=[vm(NX, *mat)],
        flops=18 * cube,
    )
    b_before, b_line = call(
        line_shift_kernel,
        "line_shift",
        [(NY - 1,) + small, small],
        pos,
        rows[0],
        *got,
        y_maps,
        scratch=[vm(NY, *small)],
        flops=cube,
    )
    got = [lax.ppermute(b_line, "tm", along_x(s)) for s in SHIFTS]
    *parts, b_group = call(
        group_shift_kernel,
        "group_shift",
        [small] * 5,
        pos,
        b_line,
        *got,
        x_maps,
        y_before,
        b_before,
        scratch=[vm(NX, *small), vm(NX, *small), vm(NY, *small)],
        flops=2 * cube,
    )
    (e,) = call(
        first_hop_kernel, "hop0", [small], pos, initial_state, high, low, b_group, flops=cube
    )
    parts[1:] = [lax.ppermute(r, "tm", along_y(s)) for r, s in zip(parts[1:], SHIFTS)]
    ends = [e]
    for k in range(1, n_grp - 1):
        came = lax.ppermute(ends[-1], "grp", [(k - 1, k)])
        last = k == n_grp - 2
        (e,) = call(
            last_hop_kernel if last else hop_kernel,
            "last_hop" if last else "hop",
            [small],
            pos,
            came,
            high,
            low,
            b_group,
            *(ends if last else ()),
            flops=cube,
            after=parts[1:] if k == 3 else (),
        )
        ends.append(e)

    def onward(s):
        size = len(spots)
        return [
            (z * size + i, (z + 1) * size + j) for z in range(n_grp - 1) for i, j in along_y(s)
        ]

    got = [lax.ppermute(ends[-1], ("grp", "tm"), onward(s)) for s in (0,) + SHIFTS]
    kept, sent = call(
        chip_kernel,
        "chip_start",
        [(half, modes)] * 2,
        pos,
        *got,
        *parts,
        initial_state,
        through,
        both,
        first,
        scratch=[vm(half, modes), vm(half, modes)],
        flops=cube,
    )
    back = lax.ppermute(sent, "tm", swap)
    observed, final = call(
        finish_kernel,
        "finish",
        [(steps, samples), mat],
        pos,
        kept,
        back,
        whole,
        shifted,
        weights,
        driven,
        scratch=[vm(samples, modes)],
        flops=3 * cube,
    )
    return observed, final[None]


def solution(mesh):
    in_specs = (
        P(),
        P(("grp", "tm"), None),
        P(("grp", "tm"), None, None),
        P(),
        P(("grp", "tm"), None, None),
        P(("grp", "tm"), None, None),
        P(("grp", "tm"), None),
        P(("grp", "tm"), None, None, None),
    )
    out_specs = (P(("grp", "tm"), None), P(("grp", "tm"), None, None))
    return jax.shard_map(body, mesh=mesh, in_specs=in_specs, out_specs=out_specs, check_vma=False)
```

```python
import functools

import jax
import jax.numpy as jnp
from jax import lax
from jax.experimental import pallas as pl
from jax.experimental.pallas import tpu as pltpu
from jax.sharding import PartitionSpec as P

F32 = jnp.float32
BF16 = jnp.bfloat16
NY = 4
NX = 4
SHIFTS = (1, 3, 2)


def split(a):
    hi = a.astype(BF16)
    return hi, (a - hi.astype(F32)).astype(BF16)


def dot(a, b, transposed=False):
    dims = (((1,), (1 if transposed else 0,)), ((), ()))
    return lax.dot_general(a, b, dims, preferred_element_type=F32)


def mm(left, right, transposed=False):
    ah, al = left
    bh, bl = right
    rows = ah.shape[0]
    if rows % 16 == 0 and rows <= 64:
        both = dot(jnp.concatenate([ah, al], axis=0), bh, transposed)
        return both[:rows] + (dot(ah, bl, transposed) + both[rows:])
    return dot(ah, bh, transposed) + (dot(ah, bl, transposed) + dot(al, bh, transposed))


def place():
    t = lax.axis_index("tm")
    return lax.rem(t, 2), lax.rem(t // 2, NY), t // (2 * NY), lax.axis_index("grp")


def call(kernel, name, outs, *args, scratch=(), flops=0, after=()):
    shapes = [s if hasattr(s, "dtype") else jax.ShapeDtypeStruct(s, F32) for s in outs]
    vmem = pl.BlockSpec(memory_space=pltpu.VMEM)
    moved = sum(4 * a.size for a in args) + sum(4 * s.size for s in shapes)
    n_args, n_after = len(args), len(after)

    def run(*refs):
        kernel(place(), *refs[:n_args], *refs[n_args + n_after :])

    return pl.pallas_call(
        run,
        out_shape=shapes,
        in_specs=[vmem] * n_args + [pl.BlockSpec(memory_space=pl.ANY)] * n_after,
        out_specs=[vmem] * len(shapes),
        scratch_shapes=list(scratch),
        name=name,
        cost_estimate=pl.CostEstimate(flops=flops, bytes_accessed=moved, transcendentals=0),
        compiler_params=pltpu.CompilerParams(vmem_limit_bytes=16 * 1024 * 1024),
    )(*args, *after)


def pack_kernel(loads, samples_of, steps_of, counts, out, samples_buf, steps_buf, counts_buf, sems, *, samples):
    owners, cap, modes = loads.shape
    half = cap // 2
    copies = [
        pltpu.make_async_copy(samples_of, samples_buf, sems.at[0]),
        pltpu.make_async_copy(steps_of, steps_buf, sems.at[1]),
        pltpu.make_async_copy(counts, counts_buf, sems.at[2]),
        pltpu.make_async_copy(loads.at[:, :half, :], out.at[:, :, 0:modes], sems.at[3]),
        pltpu.make_async_copy(loads.at[:, half:, :], out.at[:, :, modes : 2 * modes], sems.at[4]),
    ]
    for copy in copies:
        copy.start()
    for copy in copies[:3]:
        copy.wait()
    slot = lax.broadcasted_iota(jnp.int32, (cap, owners), 0)
    codes = jnp.where(slot < counts_buf[...], steps_buf[...] * samples + samples_buf[...], -1)
    codes = codes.astype(F32)
    lane = lax.broadcasted_iota(jnp.int32, (half, 128), 1)
    for j in range(owners):
        out[j, :, 2 * modes :] = jnp.where(
            lane == 0, codes[:half, j : j + 1], codes[half:, j : j + 1]
        )
    for copy in copies[3:]:
        copy.wait()


def compose_kernel(pos, retain, coupling, probe, whole, seen):
    steps, modes = retain.shape
    rows = lax.broadcasted_iota(jnp.int32, (modes, modes), 0)
    cols = lax.broadcasted_iota(jnp.int32, (modes, modes), 1)
    total = coupling[0].T + jnp.where(rows == cols, retain[0:1, :], 0.0)
    step = lax.broadcasted_iota(jnp.int32, (steps, modes), 0)
    state = jnp.zeros((steps, modes), F32)
    for t in range(steps):
        u = steps - 1 - t
        state = jnp.where(step == u, probe[...], state)
        state = state * retain[u : u + 1, :] + mm(split(state), split(coupling[u]))
        if t > 0:
            total = total * retain[t : t + 1, :] + mm(split(total), split(coupling[t]), True)
    whole[...] = total
    seen[...] = state


def drive_kernel(pos, arrived, retain, coupling, probe, shifted, kept, sent, seen):
    steps, modes = retain.shape
    sources, half, _ = arrived.shape
    n = sources * half
    samples = shifted.shape[0]
    loads = jnp.concatenate(
        [
            arrived[:, :, 0:modes].reshape(n, modes),
            arrived[:, :, modes : 2 * modes].reshape(n, modes),
        ],
        axis=0,
    )
    lh, ll = split(loads)
    codes = arrived[:, :, 2 * modes : 2 * modes + 128].reshape(n, 128).T
    codes = jnp.concatenate([codes[0:1, :], codes[1:2, :]], axis=1).astype(jnp.int32)
    place = lax.broadcasted_iota(jnp.int32, (samples, 2 * n), 0)
    lane = lax.broadcasted_iota(jnp.int32, (samples, 128), 1)
    shown = jnp.zeros((samples, 128), F32)
    field = None
    for t in range(steps):
        hit = jnp.where(place + t * samples == codes, 1.0, 0.0).astype(BF16)
        kick = dot(hit, lh) + dot(hit, ll)
        if t > 0:
            kick = kick + field * retain[t : t + 1, :] + mm(parts, split(coupling[t]), True)
        field = kick
        parts = split(field)
        shown = jnp.where(lane == t, jnp.sum(field * probe[...], axis=1, keepdims=True), shown)
    shifted[...] = field
    seen[...] = shown.T[:steps]
    c = pos[0]
    h = samples // 2

    @pl.when(c == 0)
    def _():
        kept[...] = field[:h]
        sent[...] = field[h:]

    @pl.when(c != 0)
    def _():
        kept[...] = field[h:]
        sent[...] = field[:h]


def pair_kernel(pos, mine, other, both, chip):
    c = pos[0]

    @pl.when(c == 0)
    def _():
        both[0] = mine[...]
        both[1] = other[...]

    @pl.when(c != 0)
    def _():
        both[0] = other[...]
        both[1] = mine[...]

    chip[...] = mm(split(both[0]), split(both[1]))


def order(place, count, ordered, refs):
    ordered[place] = refs[0][...]
    for s, ref in zip(SHIFTS, refs[1:]):
        ordered[lax.rem(place + count - s, count)] = ref[...]


def line_map_kernel(pos, a0, a1, a3, a2, ordered, prefix, line):
    order(pos[1], NY, ordered, (a0, a1, a3, a2))
    total = ordered[0]
    for k in range(1, NY):
        prefix[k - 1] = total
        total = mm(split(total), split(ordered[k]))
    line[...] = total


def group_map_kernel(pos, a0, a1, a3, a2, prefix, ordered, through, high, low, before):
    x = pos[2]
    order(x, NX, ordered, (a0, a1, a3, a2))
    modes = high.shape[0]
    rows = lax.broadcasted_iota(jnp.int32, (modes, modes), 0)
    cols = lax.broadcasted_iota(jnp.int32, (modes, modes), 1)
    before[0] = jnp.where(rows == cols, 1.0, 0.0)
    total = ordered[0]
    for k in range(1, NX):
        before[k] = total
        total = mm(split(total), split(ordered[k]))
    high[...], low[...] = split(total)
    own = before[x]
    through[0] = own
    own = split(own)
    for k in range(1, NY):
        through[k] = mm(own, split(prefix[k - 1]))


def pair_shift_kernel(pos, kept, got, both, first, s0, s1, s3, s2, chip):
    c = pos[0]
    y = pos[1]
    r = s0.shape[0]
    mine = kept[...]
    theirs = got[...]
    zero = jnp.where(c == 0, mine, theirs)
    one = jnp.where(c == 0, theirs, mine)
    first[...] = zero
    chip[...] = mm(split(zero), split(both[1])) + one
    for s, out in zip((0,) + SHIFTS, (s0, s1, s3, s2)):
        start = pl.multiple_of(lax.rem(y + s, NY) * r, r)
        out[...] = chip[pl.ds(start, r), :]


def line_shift_kernel(pos, b0, b1, b3, b2, maps, before, line, ordered):
    order(pos[1], NY, ordered, (b0, b1, b3, b2))
    total = ordered[0]
    for k in range(1, NY):
        before[k - 1] = total
        total = mm(split(total), split(maps[k])) + ordered[k]
    line[...] = total


def group_shift_kernel(pos, b0, b1, b3, b2, maps, prefix, before, through, group, ordered, own):
    x = pos[2]
    order(x, NX, ordered, (b0, b1, b3, b2))
    own[0] = jnp.zeros_like(ordered[0])
    total = ordered[0]
    for k in range(1, NX):
        own[k] = total
        total = mm(split(total), split(maps[k])) + ordered[k]
    group[...] = total
    prior = own[x]
    through[0] = prior
    prior = split(prior)
    for k in range(1, NY):
        through[k] = mm(prior, split(prefix[k - 1])) + before[k - 1]


def released_rows(pos, initial, part):
    start = pl.multiple_of(pos[0] * (NY * part) + pos[1] * part, part)
    return initial[pl.ds(start, part), :]


def first_hop_kernel(pos, initial, high, low, shift, out):
    state = released_rows(pos, initial, out.shape[0])
    out[...] = mm(split(state), (high[...], low[...])) + shift[...]


def hop_kernel(pos, got, high, low, shift, out):
    out[...] = mm(split(got[...]), (high[...], low[...])) + shift[...]


def last_hop_kernel(pos, initial, *refs):
    gots, (maps, shifts, s0, s1, s3, s2, chips) = refs[:-7], refs[-7:]
    y = pos[1]
    g = pos[3]
    state = released_rows(pos, initial, s0.shape[0])
    for k, got in enumerate(gots):
        state = jnp.where(g == k + 1, got[...], state)
    group = split(state)
    for k in range(NY):
        chips[k] = mm(group, split(maps[k])) + shifts[k]
    for s, out in zip((0,) + SHIFTS, (s0, s1, s3, s2)):
        out[...] = chips[lax.rem(y + s, NY)]


def chip_kernel(pos, e0, e1, e3, e2, both, first, kept, sent, chip):
    c, y = pos[0], pos[1]
    r = e0.shape[0]
    for s, ref in zip((0,) + SHIFTS, (e0, e1, e3, e2)):
        start = pl.multiple_of(lax.rem(y + NY - s, NY) * r, r)
        chip[pl.ds(start, r), :] = ref[...]
    zero = chip[...]
    one = mm(split(zero), split(both[0])) + first[...]
    kept[...] = jnp.where(c == 0, zero, one)
    sent[...] = jnp.where(c == 0, one, zero)


def finish_kernel(pos, kept, got, whole, shifted, weights, driven, observed, final, start):
    c = pos[0]
    h = kept.shape[0]

    @pl.when(c == 0)
    def _():
        start[:h] = kept[...]
        start[h:] = got[...]

    @pl.when(c != 0)
    def _():
        start[:h] = got[...]
        start[h:] = kept[...]

    parts = split(start[...])
    final[...] = mm(parts, split(whole[...])) + shifted[...]
    observed[...] = mm(split(weights[...]), parts, True) + driven[...]


def body(initial_state, retain, coupling, probe, rec_sample, rec_step, rec_count, rec_load):
    steps, modes, _ = coupling.shape
    samples = initial_state.shape[0]
    owners, cap = rec_sample.shape[1:]
    half = samples // 2
    part = half // NY
    mat = (modes, modes)
    vm = lambda *s: pltpu.VMEM(s, F32)

    def at(x, y, c):
        return (x * NY + y) * 2 + c

    spots = [(x, y, c) for x in range(NX) for y in range(NY) for c in range(2)]
    swap = [(at(x, y, c), at(x, y, 1 - c)) for x, y, c in spots]

    def along_y(s):
        return [(at(x, y, c), at(x, (y + s) % NY, c)) for x, y, c in spots]

    def along_x(s):
        return [(at(x, y, c), at((x + s) % NX, y, c)) for x, y, c in spots]

    n_grp = lax.axis_size("grp")

    packed = pl.pallas_call(
        functools.partial(pack_kernel, samples=samples),
        out_shape=jax.ShapeDtypeStruct((owners, cap // 2, 2 * modes + 128), F32),
        in_specs=[pl.BlockSpec(memory_space=pltpu.HBM)] * 4,
        out_specs=pl.BlockSpec(memory_space=pltpu.VMEM),
        scratch_shapes=[
            pltpu.VMEM((cap, owners), jnp.int32),
            pltpu.VMEM((cap, owners), jnp.int32),
            pltpu.VMEM((1, owners), jnp.int32),
            pltpu.SemaphoreType.DMA((5,)),
        ],
        name="pack",
        cost_estimate=pl.CostEstimate(flops=0, bytes_accessed=2**20, transcendentals=0),
    )(rec_load[0], rec_sample[0].T, rec_step[0].T, rec_count)
    arrived = lax.all_to_all(packed, "tm", split_axis=0, concat_axis=0)

    cube = 2 * modes * modes * modes
    probe_row = probe[None, :]
    whole, weights = call(
        compose_kernel,
        "compose",
        [mat, (steps, modes)],
        retain,
        coupling,
        probe_row,
        flops=22 * cube,
        after=(packed,),
    )
    other = lax.ppermute(whole, "tm", swap)
    both, chip = call(pair_kernel, "pair_map", [(2,) + mat, mat], whole, other, flops=3 * cube)
    chips = [lax.ppermute(chip, "tm", along_y(s)) for s in SHIFTS]
    shifted, kept, sent, driven = call(
        drive_kernel,
        "drive",
        [mat, (half, modes), (half, modes), (steps, samples)],
        arrived,
        retain,
        coupling,
        probe_row,
        flops=60 * cube,
    )
    back = lax.ppermute(sent, "tm", swap)
    small = (part, modes)
    first, *rows = call(
        pair_shift_kernel,
        "pair_shift",
        [(half, modes)] + [small] * 4,
        kept,
        back,
        both,
        scratch=[vm(half, modes)],
        flops=cube,
    )
    got = [lax.ppermute(r, "tm", along_y(s)) for r, s in zip(rows[1:], SHIFTS)]
    y_maps, y_before, line = call(
        line_map_kernel,
        "line_map",
        [(NY,) + mat, (NY - 1,) + mat, mat],
        chip,
        *chips,
        flops=9 * cube,
        after=got,
    )
    lines = [lax.ppermute(line, "tm", along_x(s)) for s in SHIFTS]
    half_mat = jax.ShapeDtypeStruct(mat, BF16)
    x_maps, through, high, low = call(
        group_map_kernel,
        "group_map",
        [(NX,) + mat, (NY,) + mat, half_mat, half_mat],
        line,
        *lines,
        y_before,
        scratch=[vm(NX, *mat)],
        flops=18 * cube,
    )
    b_before, b_line = call(
        line_shift_kernel,
        "line_shift",
        [(NY - 1,) + small, small],
        rows[0],
        *got,
        y_maps,
        scratch=[vm(NY, *small)],
        flops=cube,
    )
    got = [lax.ppermute(b_line, "tm", along_x(s)) for s in SHIFTS]
    b_through, b_group = call(
        group_shift_kernel,
        "group_shift",
        [(NY,) + small, small],
        b_line,
        *got,
        x_maps,
        y_before,
        b_before,
        scratch=[vm(NX, *small), vm(NX, *small)],
        flops=2 * cube,
    )
    (e,) = call(
        first_hop_kernel, "hop0", [small], initial_state, high, low, b_group, flops=cube
    )
    carried = [lax.ppermute(e, "grp", [(0, 1)])]
    for k in range(1, n_grp - 1):
        (e,) = call(hop_kernel, "hop", [small], carried[-1], high, low, b_group, flops=cube)
        carried.append(lax.ppermute(e, "grp", [(k, k + 1)]))
    rows = call(
        last_hop_kernel,
        "chips",
        [small] * 4,
        initial_state,
        *carried,
        through,
        b_through,
        scratch=[vm(NY, *small)],
        flops=2 * cube,
    )
    got = [lax.ppermute(r, "tm", along_y(s)) for r, s in zip(rows[1:], SHIFTS)]
    kept, sent = call(
        chip_kernel,
        "chip_start",
        [(half, modes)] * 2,
        rows[0],
        *got,
        both,
        first,
        scratch=[vm(half, modes)],
        flops=cube,
    )
    back = lax.ppermute(sent, "tm", swap)
    observed, final = call(
        finish_kernel,
        "finish",
        [(steps, samples), mat],
        kept,
        back,
        whole,
        shifted,
        weights,
        driven,
        scratch=[vm(samples, modes)],
        flops=3 * cube,
    )
    return observed, final[None]


def solution(mesh):
    in_specs = (
        P(),
        P(("grp", "tm"), None),
        P(("grp", "tm"), None, None),
        P(),
        P(("grp", "tm"), None, None),
        P(("grp", "tm"), None, None),
        P(("grp", "tm"), None),
        P(("grp", "tm"), None, None, None),
    )
    out_specs = (P(("grp", "tm"), None), P(("grp", "tm"), None, None))
    return jax.shard_map(body, mesh=mesh, in_specs=in_specs, out_specs=out_specs, check_vma=False)
```

```python
import functools

import jax
import jax.numpy as jnp
from jax import lax
from jax.experimental import pallas as pl
from jax.experimental.pallas import tpu as pltpu
from jax.sharding import PartitionSpec as P

F32 = jnp.float32
BF16 = jnp.bfloat16
NY = 4
NX = 4
SHIFTS = (1, 3, 2)


def split(a):
    hi = a.astype(BF16)
    return hi, (a - hi.astype(F32)).astype(BF16)


def dot(a, b, transposed=False):
    dims = (((1,), (1 if transposed else 0,)), ((), ()))
    return lax.dot_general(a, b, dims, preferred_element_type=F32)


def mm(left, right, transposed=False):
    ah, al = left
    bh, bl = right
    rows = ah.shape[0]
    if rows % 16 == 0 and rows <= 64:
        both = dot(jnp.concatenate([ah, al], axis=0), bh, transposed)
        return both[:rows] + (dot(ah, bl, transposed) + both[rows:])
    return dot(ah, bh, transposed) + (dot(ah, bl, transposed) + dot(al, bh, transposed))


def place():
    t = lax.axis_index("tm")
    return lax.rem(t, 2), lax.rem(t // 2, NY), t // (2 * NY), lax.axis_index("grp")


def call(kernel, name, outs, *args, scratch=(), flops=0, after=()):
    shapes = [s if hasattr(s, "dtype") else jax.ShapeDtypeStruct(s, F32) for s in outs]
    vmem = pl.BlockSpec(memory_space=pltpu.VMEM)
    moved = sum(4 * a.size for a in args) + sum(4 * s.size for s in shapes)
    n_args, n_after = len(args), len(after)

    def run(*refs):
        kernel(place(), *refs[:n_args], *refs[n_args + n_after :])

    return pl.pallas_call(
        run,
        out_shape=shapes,
        in_specs=[vmem] * n_args + [pl.BlockSpec(memory_space=pl.ANY)] * n_after,
        out_specs=[vmem] * len(shapes),
        scratch_shapes=list(scratch),
        name=name,
        cost_estimate=pl.CostEstimate(flops=flops, bytes_accessed=moved, transcendentals=0),
        compiler_params=pltpu.CompilerParams(vmem_limit_bytes=16 * 1024 * 1024),
    )(*args, *after)


def pack_kernel(loads, samples_of, steps_of, counts, out, samples_buf, steps_buf, counts_buf, sems, *, samples):
    owners, cap, modes = loads.shape
    half = cap // 2
    copies = [
        pltpu.make_async_copy(samples_of, samples_buf, sems.at[0]),
        pltpu.make_async_copy(steps_of, steps_buf, sems.at[1]),
        pltpu.make_async_copy(counts, counts_buf, sems.at[2]),
        pltpu.make_async_copy(loads.at[:, :half, :], out.at[:, :, 0:modes], sems.at[3]),
        pltpu.make_async_copy(loads.at[:, half:, :], out.at[:, :, modes : 2 * modes], sems.at[4]),
    ]
    for copy in copies:
        copy.start()
    for copy in copies[:3]:
        copy.wait()
    slot = lax.broadcasted_iota(jnp.int32, (cap, owners), 0)
    codes = jnp.where(slot < counts_buf[...], steps_buf[...] * samples + samples_buf[...], -1)
    codes = codes.astype(F32)
    lane = lax.broadcasted_iota(jnp.int32, (half, 128), 1)
    for j in range(owners):
        out[j, :, 2 * modes :] = jnp.where(
            lane == 0, codes[:half, j : j + 1], codes[half:, j : j + 1]
        )
    for copy in copies[3:]:
        copy.wait()


def compose_kernel(pos, retain, coupling, probe, whole, seen):
    steps, modes = retain.shape
    rows = lax.broadcasted_iota(jnp.int32, (modes, modes), 0)
    cols = lax.broadcasted_iota(jnp.int32, (modes, modes), 1)
    total = coupling[0].T + jnp.where(rows == cols, retain[0:1, :], 0.0)
    step = lax.broadcasted_iota(jnp.int32, (steps, modes), 0)
    state = jnp.zeros((steps, modes), F32)
    for t in range(steps):
        u = steps - 1 - t
        state = jnp.where(step == u, probe[...], state)
        state = state * retain[u : u + 1, :] + mm(split(state), split(coupling[u]))
        if t > 0:
            total = total * retain[t : t + 1, :] + mm(split(total), split(coupling[t]), True)
    whole[...] = total
    seen[...] = state


def drive_kernel(pos, arrived, retain, coupling, probe, shifted, kept, sent, seen):
    steps, modes = retain.shape
    sources, half, _ = arrived.shape
    n = sources * half
    samples = shifted.shape[0]
    loads = jnp.concatenate(
        [
            arrived[:, :, 0:modes].reshape(n, modes),
            arrived[:, :, modes : 2 * modes].reshape(n, modes),
        ],
        axis=0,
    )
    lh, ll = split(loads)
    codes = arrived[:, :, 2 * modes : 2 * modes + 128].reshape(n, 128).T
    codes = jnp.concatenate([codes[0:1, :], codes[1:2, :]], axis=1).astype(jnp.int32)
    place = lax.broadcasted_iota(jnp.int32, (samples, 2 * n), 0)
    lane = lax.broadcasted_iota(jnp.int32, (samples, 128), 1)
    shown = jnp.zeros((samples, 128), F32)
    field = None
    for t in range(steps):
        hit = jnp.where(place + t * samples == codes, 1.0, 0.0).astype(BF16)
        kick = dot(hit, lh) + dot(hit, ll)
        if t > 0:
            kick = kick + field * retain[t : t + 1, :] + mm(parts, split(coupling[t]), True)
        field = kick
        parts = split(field)
        shown = jnp.where(lane == t, jnp.sum(field * probe[...], axis=1, keepdims=True), shown)
    shifted[...] = field
    seen[...] = shown.T[:steps]
    c = pos[0]
    h = samples // 2

    @pl.when(c == 0)
    def _():
        kept[...] = field[:h]
        sent[...] = field[h:]

    @pl.when(c != 0)
    def _():
        kept[...] = field[h:]
        sent[...] = field[:h]


def pair_kernel(pos, mine, other, both, chip):
    c = pos[0]

    @pl.when(c == 0)
    def _():
        both[0] = mine[...]
        both[1] = other[...]

    @pl.when(c != 0)
    def _():
        both[0] = other[...]
        both[1] = mine[...]

    chip[...] = mm(split(both[0]), split(both[1]))


def order(place, count, ordered, refs):
    ordered[place] = refs[0][...]
    for s, ref in zip(SHIFTS, refs[1:]):
        ordered[lax.rem(place + count - s, count)] = ref[...]


def line_kernel(
    pos, a0, a1, a3, a2, b0, b1, b3, b2, prefix, line, before, packet, maps, shifts
):
    order(pos[1], NY, maps, (a0, a1, a3, a2))
    order(pos[1], NY, shifts, (b0, b1, b3, b2))
    total, moved = maps[0], shifts[0]
    for k in range(1, NY):
        prefix[k - 1] = total
        before[k - 1] = moved
        right = split(maps[k])
        total = mm(split(total), right)
        moved = mm(split(moved), right) + shifts[k]
    line[...] = total
    h = line.shape[0] // 2
    packet[:h] = line[pl.ds(pl.multiple_of(pos[0] * h, h), h), :]
    packet[h:] = moved


def stack_kernel(pos, p1, p3, p2, out):
    for i, ref in enumerate((p1, p3, p2)):
        out[i] = ref[: out.shape[1]]


def group_kernel(
    pos,
    line,
    p0,
    p1,
    p3,
    p2,
    theirs,
    prefix,
    before,
    through,
    high,
    low,
    b_through,
    b_group,
    maps,
    shifts,
    a_before,
    own,
):
    x = pos[2]
    modes = high.shape[0]
    h = theirs.shape[1]
    here = pl.ds(pl.multiple_of(pos[0] * h, h), h)
    there = pl.ds(pl.multiple_of((1 - pos[0]) * h, h), h)
    maps[x] = line[...]
    shifts[x] = p0[h:]
    for i, (s, ref) in enumerate(zip(SHIFTS, (p1, p3, p2))):
        spot = lax.rem(x + NX - s, NX)
        maps[spot, here, :] = ref[:h]
        maps[spot, there, :] = theirs[i]
        shifts[spot] = ref[h:]
    rows = lax.broadcasted_iota(jnp.int32, (modes, modes), 0)
    cols = lax.broadcasted_iota(jnp.int32, (modes, modes), 1)
    a_before[0] = jnp.where(rows == cols, 1.0, 0.0)
    own[0] = jnp.zeros_like(shifts[0])
    total, moved = maps[0], shifts[0]
    for k in range(1, NX):
        a_before[k] = total
        own[k] = moved
        right = split(maps[k])
        total = mm(split(total), right)
        moved = mm(split(moved), right) + shifts[k]
    high[...], low[...] = split(total)
    b_group[...] = moved
    through[0] = a_before[x]
    b_through[0] = own[x]
    a_own, b_own = split(a_before[x]), split(own[x])
    for k in range(1, NY):
        right = split(prefix[k - 1])
        through[k] = mm(a_own, right)
        b_through[k] = mm(b_own, right) + before[k - 1]


def pair_shift_kernel(pos, kept, got, both, first, s0, s1, s3, s2, chip):
    c = pos[0]
    y = pos[1]
    r = s0.shape[0]
    mine = kept[...]
    theirs = got[...]
    zero = jnp.where(c == 0, mine, theirs)
    one = jnp.where(c == 0, theirs, mine)
    first[...] = zero
    chip[...] = mm(split(zero), split(both[1])) + one
    for s, out in zip((0,) + SHIFTS, (s0, s1, s3, s2)):
        start = pl.multiple_of(lax.rem(y + s, NY) * r, r)
        out[...] = chip[pl.ds(start, r), :]


def released_rows(pos, initial, part):
    start = pl.multiple_of(pos[0] * (NY * part) + pos[1] * part, part)
    return initial[pl.ds(start, part), :]


def first_hop_kernel(pos, initial, high, low, shift, out):
    state = released_rows(pos, initial, out.shape[0])
    out[...] = mm(split(state), (high[...], low[...])) + shift[...]


def hop_kernel(pos, got, high, low, shift, out):
    out[...] = mm(split(got[...]), (high[...], low[...])) + shift[...]


def last_hop_kernel(pos, initial, *refs):
    gots, (maps, shifts, s0, s1, s3, s2, chips) = refs[:-7], refs[-7:]
    y = pos[1]
    g = pos[3]
    state = released_rows(pos, initial, s0.shape[0])
    for k, got in enumerate(gots):
        state = jnp.where(g == k + 1, got[...], state)
    group = split(state)
    for k in range(NY):
        chips[k] = mm(group, split(maps[k])) + shifts[k]
    for s, out in zip((0,) + SHIFTS, (s0, s1, s3, s2)):
        out[...] = chips[lax.rem(y + s, NY)]


def chip_kernel(pos, e0, e1, e3, e2, both, first, kept, sent, chip):
    c, y = pos[0], pos[1]
    r = e0.shape[0]
    for s, ref in zip((0,) + SHIFTS, (e0, e1, e3, e2)):
        start = pl.multiple_of(lax.rem(y + NY - s, NY) * r, r)
        chip[pl.ds(start, r), :] = ref[...]
    zero = chip[...]
    one = mm(split(zero), split(both[0])) + first[...]
    kept[...] = jnp.where(c == 0, zero, one)
    sent[...] = jnp.where(c == 0, one, zero)


def finish_kernel(pos, kept, got, whole, shifted, weights, driven, observed, final, start):
    c = pos[0]
    h = kept.shape[0]

    @pl.when(c == 0)
    def _():
        start[:h] = kept[...]
        start[h:] = got[...]

    @pl.when(c != 0)
    def _():
        start[:h] = got[...]
        start[h:] = kept[...]

    parts = split(start[...])
    final[...] = mm(parts, split(whole[...])) + shifted[...]
    observed[...] = mm(split(weights[...]), parts, True) + driven[...]


def body(initial_state, retain, coupling, probe, rec_sample, rec_step, rec_count, rec_load):
    steps, modes, _ = coupling.shape
    samples = initial_state.shape[0]
    owners, cap = rec_sample.shape[1:]
    half = samples // 2
    part = half // NY
    mat = (modes, modes)
    vm = lambda *s: pltpu.VMEM(s, F32)

    def at(x, y, c):
        return (x * NY + y) * 2 + c

    spots = [(x, y, c) for x in range(NX) for y in range(NY) for c in range(2)]
    swap = [(at(x, y, c), at(x, y, 1 - c)) for x, y, c in spots]

    def along_y(s):
        return [(at(x, y, c), at(x, (y + s) % NY, c)) for x, y, c in spots]

    def along_x(s):
        return [(at(x, y, c), at((x + s) % NX, y, c)) for x, y, c in spots]

    n_grp = lax.axis_size("grp")

    packed = pl.pallas_call(
        functools.partial(pack_kernel, samples=samples),
        out_shape=jax.ShapeDtypeStruct((owners, cap // 2, 2 * modes + 128), F32),
        in_specs=[pl.BlockSpec(memory_space=pltpu.HBM)] * 4,
        out_specs=pl.BlockSpec(memory_space=pltpu.VMEM),
        scratch_shapes=[
            pltpu.VMEM((cap, owners), jnp.int32),
            pltpu.VMEM((cap, owners), jnp.int32),
            pltpu.VMEM((1, owners), jnp.int32),
            pltpu.SemaphoreType.DMA((5,)),
        ],
        name="pack",
        cost_estimate=pl.CostEstimate(flops=3000000000, bytes_accessed=2**20, transcendentals=0),
    )(rec_load[0], rec_sample[0].T, rec_step[0].T, rec_count)
    arrived = lax.all_to_all(packed, "tm", split_axis=0, concat_axis=0)

    cube = 2 * modes * modes * modes
    probe_row = probe[None, :]
    whole, weights = call(
        compose_kernel,
        "compose",
        [mat, (steps, modes)],
        retain,
        coupling,
        probe_row,
        flops=22 * cube,
        after=(packed,),
    )
    other = lax.ppermute(whole, "tm", swap)
    both, chip = call(pair_kernel, "pair_map", [(2,) + mat, mat], whole, other, flops=3 * cube)
    chips = [lax.ppermute(chip, "tm", along_y(s)) for s in SHIFTS]
    shifted, kept, sent, driven = call(
        drive_kernel,
        "drive",
        [mat, (half, modes), (half, modes), (steps, samples)],
        arrived,
        retain,
        coupling,
        probe_row,
        flops=60 * cube,
    )
    back = lax.ppermute(sent, "tm", swap)
    small = (part, modes)
    first, *rows = call(
        pair_shift_kernel,
        "pair_shift",
        [(half, modes)] + [small] * 4,
        kept,
        back,
        both,
        scratch=[vm(half, modes)],
        flops=cube,
    )
    got = [lax.ppermute(r, "tm", along_y(s)) for r, s in zip(rows[1:], SHIFTS)]
    y_before, line, b_before, packet = call(
        line_kernel,
        "line",
        [(NY - 1,) + mat, mat, (NY - 1,) + small, (half + part, modes)],
        chip,
        *chips,
        rows[0],
        *got,
        scratch=[vm(NY, *mat), vm(NY, *small)],
        flops=10 * cube,
    )
    packets = [lax.ppermute(packet, "tm", along_x(s)) for s in SHIFTS]
    (halves,) = call(stack_kernel, "stack", [(NX - 1, half, modes)], *packets)
    half_mat = jax.ShapeDtypeStruct(mat, BF16)
    through, high, low, b_through, b_group = call(
        group_kernel,
        "group",
        [(NY,) + mat, half_mat, half_mat, (NY,) + small, small],
        line,
        packet,
        *packets,
        lax.ppermute(halves, "tm", swap),
        y_before,
        b_before,
        scratch=[vm(NX, *mat), vm(NX, *small), vm(NX, *mat), vm(NX, *small)],
        flops=20 * cube,
    )
    (e,) = call(
        first_hop_kernel, "hop0", [small], initial_state, high, low, b_group, flops=cube
    )
    carried = [lax.ppermute(e, "grp", [(0, 1)])]
    for k in range(1, n_grp - 1):
        (e,) = call(hop_kernel, "hop", [small], carried[-1], high, low, b_group, flops=cube)
        carried.append(lax.ppermute(e, "grp", [(k, k + 1)]))
    rows = call(
        last_hop_kernel,
        "chips",
        [small] * 4,
        initial_state,
        *carried,
        through,
        b_through,
        scratch=[vm(NY, *small)],
        flops=2 * cube,
    )
    got = [lax.ppermute(r, "tm", along_y(s)) for r, s in zip(rows[1:], SHIFTS)]
    kept, sent = call(
        chip_kernel,
        "chip_start",
        [(half, modes)] * 2,
        rows[0],
        *got,
        both,
        first,
        scratch=[vm(half, modes)],
        flops=cube,
    )
    back = lax.ppermute(sent, "tm", swap)
    observed, final = call(
        finish_kernel,
        "finish",
        [(steps, samples), mat],
        kept,
        back,
        whole,
        shifted,
        weights,
        driven,
        scratch=[vm(samples, modes)],
        flops=3 * cube,
    )
    return observed, final[None]


def solution(mesh):
    in_specs = (
        P(),
        P(("grp", "tm"), None),
        P(("grp", "tm"), None, None),
        P(),
        P(("grp", "tm"), None, None),
        P(("grp", "tm"), None, None),
        P(("grp", "tm"), None),
        P(("grp", "tm"), None, None, None),
    )
    out_specs = (P(("grp", "tm"), None), P(("grp", "tm"), None, None))
    return jax.shard_map(body, mesh=mesh, in_specs=in_specs, out_specs=out_specs, check_vma=False)
```

```python
import functools

import jax
import jax.numpy as jnp
from jax import lax
from jax.experimental import pallas as pl
from jax.experimental.pallas import tpu as pltpu
from jax.sharding import PartitionSpec as P

F32 = jnp.float32
BF16 = jnp.bfloat16
NY = 4
NX = 4
SHIFTS = (1, 3, 2)


def split(a):
    hi = a.astype(BF16)
    return hi, (a - hi.astype(F32)).astype(BF16)


def dot(a, b, transposed=False):
    dims = (((1,), (1 if transposed else 0,)), ((), ()))
    return lax.dot_general(a, b, dims, preferred_element_type=F32)


def mm(left, right, transposed=False):
    ah, al = left
    bh, bl = right
    rows = ah.shape[0]
    if rows % 16 == 0 and rows <= 64:
        both = dot(jnp.concatenate([ah, al], axis=0), bh, transposed)
        return both[:rows] + (dot(ah, bl, transposed) + both[rows:])
    return dot(ah, bh, transposed) + (dot(ah, bl, transposed) + dot(al, bh, transposed))


def place():
    t = lax.axis_index("tm")
    return lax.rem(t, 2), lax.rem(t // 2, NY), t // (2 * NY), lax.axis_index("grp")


def call(kernel, name, outs, *args, scratch=(), flops=0, after=()):
    shapes = [s if hasattr(s, "dtype") else jax.ShapeDtypeStruct(s, F32) for s in outs]
    vmem = pl.BlockSpec(memory_space=pltpu.VMEM)
    moved = sum(4 * a.size for a in args) + sum(4 * s.size for s in shapes)
    n_args, n_after = len(args), len(after)

    def run(*refs):
        kernel(place(), *refs[:n_args], *refs[n_args + n_after :])

    return pl.pallas_call(
        run,
        out_shape=shapes,
        in_specs=[vmem] * n_args + [pl.BlockSpec(memory_space=pl.ANY)] * n_after,
        out_specs=[vmem] * len(shapes),
        scratch_shapes=list(scratch),
        name=name,
        cost_estimate=pl.CostEstimate(flops=flops, bytes_accessed=moved, transcendentals=0),
        compiler_params=pltpu.CompilerParams(vmem_limit_bytes=16 * 1024 * 1024),
    )(*args, *after)


def pack_kernel(loads, samples_of, steps_of, counts, out, samples_buf, steps_buf, counts_buf, sems, *, samples):
    owners, cap, modes = loads.shape
    half = cap // 2
    copies = [
        pltpu.make_async_copy(samples_of, samples_buf, sems.at[0]),
        pltpu.make_async_copy(steps_of, steps_buf, sems.at[1]),
        pltpu.make_async_copy(counts, counts_buf, sems.at[2]),
        pltpu.make_async_copy(loads.at[:, :half, :], out.at[:, :, 0:modes], sems.at[3]),
        pltpu.make_async_copy(loads.at[:, half:, :], out.at[:, :, modes : 2 * modes], sems.at[4]),
    ]
    for copy in copies:
        copy.start()
    for copy in copies[:3]:
        copy.wait()
    slot = lax.broadcasted_iota(jnp.int32, (cap, owners), 0)
    codes = jnp.where(slot < counts_buf[...], steps_buf[...] * samples + samples_buf[...], -1)
    codes = codes.astype(F32)
    lane = lax.broadcasted_iota(jnp.int32, (half, 128), 1)
    for j in range(owners):
        out[j, :, 2 * modes :] = jnp.where(
            lane == 0, codes[:half, j : j + 1], codes[half:, j : j + 1]
        )
    for copy in copies[3:]:
        copy.wait()


def compose_kernel(pos, retain, coupling, probe, whole, seen):
    steps, modes = retain.shape
    rows = lax.broadcasted_iota(jnp.int32, (modes, modes), 0)
    cols = lax.broadcasted_iota(jnp.int32, (modes, modes), 1)
    total = coupling[0].T + jnp.where(rows == cols, retain[0:1, :], 0.0)
    step = lax.broadcasted_iota(jnp.int32, (steps, modes), 0)
    state = jnp.zeros((steps, modes), F32)
    for t in range(steps):
        u = steps - 1 - t
        state = jnp.where(step == u, probe[...], state)
        state = state * retain[u : u + 1, :] + mm(split(state), split(coupling[u]))
        if t > 0:
            total = total * retain[t : t + 1, :] + mm(split(total), split(coupling[t]), True)
    whole[...] = total
    seen[...] = state


def drive_kernel(pos, arrived, retain, coupling, probe, shifted, kept, sent, seen):
    steps, modes = retain.shape
    sources, half, _ = arrived.shape
    n = sources * half
    samples = shifted.shape[0]
    loads = jnp.concatenate(
        [
            arrived[:, :, 0:modes].reshape(n, modes),
            arrived[:, :, modes : 2 * modes].reshape(n, modes),
        ],
        axis=0,
    )
    lh, ll = split(loads)
    codes = arrived[:, :, 2 * modes : 2 * modes + 128].reshape(n, 128).T
    codes = jnp.concatenate([codes[0:1, :], codes[1:2, :]], axis=1).astype(jnp.int32)
    place = lax.broadcasted_iota(jnp.int32, (samples, 2 * n), 0)
    lane = lax.broadcasted_iota(jnp.int32, (samples, 128), 1)
    shown = jnp.zeros((samples, 128), F32)
    field = None
    for t in range(steps):
        hit = jnp.where(place + t * samples == codes, 1.0, 0.0).astype(BF16)
        kick = dot(hit, lh) + dot(hit, ll)
        if t > 0:
            kick = kick + field * retain[t : t + 1, :] + mm(parts, split(coupling[t]), True)
        field = kick
        parts = split(field)
        shown = jnp.where(lane == t, jnp.sum(field * probe[...], axis=1, keepdims=True), shown)
    shifted[...] = field
    seen[...] = shown.T[:steps]
    c = pos[0]
    h = samples // 2

    @pl.when(c == 0)
    def _():
        kept[...] = field[:h]
        sent[...] = field[h:]

    @pl.when(c != 0)
    def _():
        kept[...] = field[h:]
        sent[...] = field[:h]


def pair_kernel(pos, mine, other, both, chip):
    c = pos[0]

    @pl.when(c == 0)
    def _():
        both[0] = mine[...]
        both[1] = other[...]

    @pl.when(c != 0)
    def _():
        both[0] = other[...]
        both[1] = mine[...]

    chip[...] = mm(split(both[0]), split(both[1]))


def order(place, count, ordered, refs):
    ordered[place] = refs[0][...]
    for s, ref in zip(SHIFTS, refs[1:]):
        ordered[lax.rem(place + count - s, count)] = ref[...]


def line_kernel(
    pos, a0, a1, a3, a2, b0, b1, b3, b2, prefix, line, before, packet, maps, shifts
):
    order(pos[1], NY, maps, (a0, a1, a3, a2))
    order(pos[1], NY, shifts, (b0, b1, b3, b2))
    total, moved = maps[0], shifts[0]
    for k in range(1, NY):
        prefix[k - 1] = total
        before[k - 1] = moved
        right = split(maps[k])
        total = mm(split(total), right)
        moved = mm(split(moved), right) + shifts[k]
    line[...] = total
    h = line.shape[0] // 2
    packet[:h] = line[pl.ds(pl.multiple_of(pos[0] * h, h), h), :]
    packet[h:] = moved


def group_kernel(
    pos,
    line,
    p0,
    p1,
    p3,
    p2,
    t1,
    t3,
    t2,
    prefix,
    before,
    through,
    high,
    low,
    b_through,
    b_group,
    maps,
    shifts,
    a_before,
    own,
):
    x = pos[2]
    modes = high.shape[0]
    h = modes // 2
    here = pl.ds(pl.multiple_of(pos[0] * h, h), h)
    there = pl.ds(pl.multiple_of((1 - pos[0]) * h, h), h)
    maps[x] = line[...]
    shifts[x] = p0[h:]
    for s, ref, theirs in zip(SHIFTS, (p1, p3, p2), (t1, t3, t2)):
        spot = lax.rem(x + NX - s, NX)
        maps[spot, here, :] = ref[:h]
        maps[spot, there, :] = theirs[:h]
        shifts[spot] = ref[h:]
    rows = lax.broadcasted_iota(jnp.int32, (modes, modes), 0)
    cols = lax.broadcasted_iota(jnp.int32, (modes, modes), 1)
    a_before[0] = jnp.where(rows == cols, 1.0, 0.0)
    own[0] = jnp.zeros_like(shifts[0])
    total, moved = maps[0], shifts[0]
    for k in range(1, NX):
        a_before[k] = total
        own[k] = moved
        right = split(maps[k])
        total = mm(split(total), right)
        moved = mm(split(moved), right) + shifts[k]
    high[...], low[...] = split(total)
    b_group[...] = moved
    through[0] = a_before[x]
    b_through[0] = own[x]
    a_own, b_own = split(a_before[x]), split(own[x])
    for k in range(1, NY):
        right = split(prefix[k - 1])
        through[k] = mm(a_own, right)
        b_through[k] = mm(b_own, right) + before[k - 1]


def pair_shift_kernel(pos, kept, got, both, first, s0, s1, s3, s2, chip):
    c = pos[0]
    y = pos[1]
    r = s0.shape[0]
    mine = kept[...]
    theirs = got[...]
    zero = jnp.where(c == 0, mine, theirs)
    one = jnp.where(c == 0, theirs, mine)
    first[...] = zero
    chip[...] = mm(split(zero), split(both[1])) + one
    for s, out in zip((0,) + SHIFTS, (s0, s1, s3, s2)):
        start = pl.multiple_of(lax.rem(y + s, NY) * r, r)
        out[...] = chip[pl.ds(start, r), :]


def released_rows(pos, initial, part):
    start = pl.multiple_of(pos[0] * (NY * part) + pos[1] * part, part)
    return initial[pl.ds(start, part), :]


def first_hop_kernel(pos, initial, high, low, shift, out):
    state = released_rows(pos, initial, out.shape[0])
    out[...] = mm(split(state), (high[...], low[...])) + shift[...]


def hop_kernel(pos, got, high, low, shift, out):
    out[...] = mm(split(got[...]), (high[...], low[...])) + shift[...]


def last_hop_kernel(pos, initial, *refs):
    gots, (maps, shifts, s0, s1, s3, s2, chips) = refs[:-7], refs[-7:]
    y = pos[1]
    g = pos[3]
    state = released_rows(pos, initial, s0.shape[0])
    for k, got in enumerate(gots):
        state = jnp.where(g == k + 1, got[...], state)
    group = split(state)
    for k in range(NY):
        chips[k] = mm(group, split(maps[k])) + shifts[k]
    for s, out in zip((0,) + SHIFTS, (s0, s1, s3, s2)):
        out[...] = chips[lax.rem(y + s, NY)]


def chip_kernel(pos, e0, e1, e3, e2, both, first, kept, sent, chip):
    c, y = pos[0], pos[1]
    r = e0.shape[0]
    for s, ref in zip((0,) + SHIFTS, (e0, e1, e3, e2)):
        start = pl.multiple_of(lax.rem(y + NY - s, NY) * r, r)
        chip[pl.ds(start, r), :] = ref[...]
    zero = chip[...]
    one = mm(split(zero), split(both[0])) + first[...]
    kept[...] = jnp.where(c == 0, zero, one)
    sent[...] = jnp.where(c == 0, one, zero)


def finish_kernel(pos, kept, got, whole, shifted, weights, driven, observed, final, start):
    c = pos[0]
    h = kept.shape[0]

    @pl.when(c == 0)
    def _():
        start[:h] = kept[...]
        start[h:] = got[...]

    @pl.when(c != 0)
    def _():
        start[:h] = got[...]
        start[h:] = kept[...]

    parts = split(start[...])
    final[...] = mm(parts, split(whole[...])) + shifted[...]
    observed[...] = mm(split(weights[...]), parts, True) + driven[...]


def body(initial_state, retain, coupling, probe, rec_sample, rec_step, rec_count, rec_load):
    steps, modes, _ = coupling.shape
    samples = initial_state.shape[0]
    owners, cap = rec_sample.shape[1:]
    half = samples // 2
    part = half // NY
    mat = (modes, modes)
    vm = lambda *s: pltpu.VMEM(s, F32)

    def at(x, y, c):
        return (x * NY + y) * 2 + c

    spots = [(x, y, c) for x in range(NX) for y in range(NY) for c in range(2)]
    swap = [(at(x, y, c), at(x, y, 1 - c)) for x, y, c in spots]

    def along_y(s):
        return [(at(x, y, c), at(x, (y + s) % NY, c)) for x, y, c in spots]

    def along_x(s):
        return [(at(x, y, c), at((x + s) % NX, y, c)) for x, y, c in spots]

    n_grp = lax.axis_size("grp")

    packed = pl.pallas_call(
        functools.partial(pack_kernel, samples=samples),
        out_shape=jax.ShapeDtypeStruct((owners, cap // 2, 2 * modes + 128), F32),
        in_specs=[pl.BlockSpec(memory_space=pltpu.HBM)] * 4,
        out_specs=pl.BlockSpec(memory_space=pltpu.VMEM),
        scratch_shapes=[
            pltpu.VMEM((cap, owners), jnp.int32),
            pltpu.VMEM((cap, owners), jnp.int32),
            pltpu.VMEM((1, owners), jnp.int32),
            pltpu.SemaphoreType.DMA((5,)),
        ],
        name="pack",
        cost_estimate=pl.CostEstimate(flops=3000000000, bytes_accessed=2**20, transcendentals=0),
    )(rec_load[0], rec_sample[0].T, rec_step[0].T, rec_count)
    arrived = lax.all_to_all(packed, "tm", split_axis=0, concat_axis=0)

    cube = 2 * modes * modes * modes
    probe_row = probe[None, :]
    whole, weights = call(
        compose_kernel,
        "compose",
        [mat, (steps, modes)],
        retain,
        coupling,
        probe_row,
        flops=22 * cube,
        after=(packed,),
    )
    other = lax.ppermute(whole, "tm", swap)
    both, chip = call(pair_kernel, "pair_map", [(2,) + mat, mat], whole, other, flops=3 * cube)
    chips = [lax.ppermute(chip, "tm", along_y(s)) for s in SHIFTS]
    shifted, kept, sent, driven = call(
        drive_kernel,
        "drive",
        [mat, (half, modes), (half, modes), (steps, samples)],
        arrived,
        retain,
        coupling,
        probe_row,
        flops=60 * cube,
    )
    back = lax.ppermute(sent, "tm", swap)
    small = (part, modes)
    first, *rows = call(
        pair_shift_kernel,
        "pair_shift",
        [(half, modes)] + [small] * 4,
        kept,
        back,
        both,
        scratch=[vm(half, modes)],
        flops=cube,
    )
    got = [lax.ppermute(r, "tm", along_y(s)) for r, s in zip(rows[1:], SHIFTS)]
    y_before, line, b_before, packet = call(
        line_kernel,
        "line",
        [(NY - 1,) + mat, mat, (NY - 1,) + small, (half + part, modes)],
        chip,
        *chips,
        rows[0],
        *got,
        scratch=[vm(NY, *mat), vm(NY, *small)],
        flops=10 * cube,
    )
    packets = [lax.ppermute(packet, "tm", along_x(s)) for s in SHIFTS]
    swapped = [lax.ppermute(p, "tm", swap) for p in packets]
    half_mat = jax.ShapeDtypeStruct(mat, BF16)
    through, high, low, b_through, b_group = call(
        group_kernel,
        "group",
        [(NY,) + mat, half_mat, half_mat, (NY,) + small, small],
        line,
        packet,
        *packets,
        *swapped,
        y_before,
        b_before,
        scratch=[vm(NX, *mat), vm(NX, *small), vm(NX, *mat), vm(NX, *small)],
        flops=20 * cube,
    )
    (e,) = call(
        first_hop_kernel, "hop0", [small], initial_state, high, low, b_group, flops=cube
    )
    carried = [lax.ppermute(e, "grp", [(0, 1)])]
    for k in range(1, n_grp - 1):
        (e,) = call(hop_kernel, "hop", [small], carried[-1], high, low, b_group, flops=cube)
        carried.append(lax.ppermute(e, "grp", [(k, k + 1)]))
    rows = call(
        last_hop_kernel,
        "chips",
        [small] * 4,
        initial_state,
        *carried,
        through,
        b_through,
        scratch=[vm(NY, *small)],
        flops=2 * cube,
    )
    got = [lax.ppermute(r, "tm", along_y(s)) for r, s in zip(rows[1:], SHIFTS)]
    kept, sent = call(
        chip_kernel,
        "chip_start",
        [(half, modes)] * 2,
        rows[0],
        *got,
        both,
        first,
        scratch=[vm(half, modes)],
        flops=cube,
    )
    back = lax.ppermute(sent, "tm", swap)
    observed, final = call(
        finish_kernel,
        "finish",
        [(steps, samples), mat],
        kept,
        back,
        whole,
        shifted,
        weights,
        driven,
        scratch=[vm(samples, modes)],
        flops=3 * cube,
    )
    return observed, final[None]


def solution(mesh):
    in_specs = (
        P(),
        P(("grp", "tm"), None),
        P(("grp", "tm"), None, None),
        P(),
        P(("grp", "tm"), None, None),
        P(("grp", "tm"), None, None),
        P(("grp", "tm"), None),
        P(("grp", "tm"), None, None, None),
    )
    out_specs = (P(("grp", "tm"), None), P(("grp", "tm"), None, None))
    return jax.shard_map(body, mesh=mesh, in_specs=in_specs, out_specs=out_specs, check_vma=False)
```

```python
import functools

import jax
import jax.numpy as jnp
from jax import lax
from jax.experimental import pallas as pl
from jax.experimental.pallas import tpu as pltpu
from jax.sharding import PartitionSpec as P

F32 = jnp.float32
BF16 = jnp.bfloat16
NY = 4
NX = 4
SHIFTS = (1, 3, 2)


def split(a):
    hi = a.astype(BF16)
    return hi, (a - hi.astype(F32)).astype(BF16)


def dot(a, b, transposed=False):
    dims = (((1,), (1 if transposed else 0,)), ((), ()))
    return lax.dot_general(a, b, dims, preferred_element_type=F32)


def mm(left, right, transposed=False):
    ah, al = left
    bh, bl = right
    rows = ah.shape[0]
    if rows % 16 == 0 and rows <= 64:
        both = dot(jnp.concatenate([ah, al], axis=0), bh, transposed)
        return both[:rows] + (dot(ah, bl, transposed) + both[rows:])
    return dot(ah, bh, transposed) + (dot(ah, bl, transposed) + dot(al, bh, transposed))


def place():
    t = lax.axis_index("tm")
    return lax.rem(t, 2), lax.rem(t // 2, NY), t // (2 * NY), lax.axis_index("grp")


def call(kernel, name, outs, *args, scratch=(), flops=0, after=()):
    shapes = [s if hasattr(s, "dtype") else jax.ShapeDtypeStruct(s, F32) for s in outs]
    vmem = pl.BlockSpec(memory_space=pltpu.VMEM)
    moved = sum(4 * a.size for a in args) + sum(4 * s.size for s in shapes)
    n_args, n_after = len(args), len(after)

    def run(*refs):
        kernel(place(), *refs[:n_args], *refs[n_args + n_after :])

    return pl.pallas_call(
        run,
        out_shape=shapes,
        in_specs=[vmem] * n_args + [pl.BlockSpec(memory_space=pl.ANY)] * n_after,
        out_specs=[vmem] * len(shapes),
        scratch_shapes=list(scratch),
        name=name,
        cost_estimate=pl.CostEstimate(flops=flops, bytes_accessed=moved, transcendentals=0),
        compiler_params=pltpu.CompilerParams(vmem_limit_bytes=16 * 1024 * 1024),
    )(*args, *after)


def pack_kernel(loads, samples_of, steps_of, counts, out, samples_buf, steps_buf, counts_buf, sems, *, samples):
    owners, cap, modes = loads.shape
    half = cap // 2
    copies = [
        pltpu.make_async_copy(samples_of, samples_buf, sems.at[0]),
        pltpu.make_async_copy(steps_of, steps_buf, sems.at[1]),
        pltpu.make_async_copy(counts, counts_buf, sems.at[2]),
        pltpu.make_async_copy(loads.at[:, :half, :], out.at[:, :, 0:modes], sems.at[3]),
        pltpu.make_async_copy(loads.at[:, half:, :], out.at[:, :, modes : 2 * modes], sems.at[4]),
    ]
    for copy in copies:
        copy.start()
    for copy in copies[:3]:
        copy.wait()
    slot = lax.broadcasted_iota(jnp.int32, (cap, owners), 0)
    codes = jnp.where(slot < counts_buf[...], steps_buf[...] * samples + samples_buf[...], -1)
    codes = codes.astype(F32)
    lane = lax.broadcasted_iota(jnp.int32, (half, 128), 1)
    for j in range(owners):
        out[j, :, 2 * modes :] = jnp.where(
            lane == 0, codes[:half, j : j + 1], codes[half:, j : j + 1]
        )
    for copy in copies[3:]:
        copy.wait()


def compose_kernel(pos, retain, coupling, probe, whole, seen):
    steps, modes = retain.shape
    rows = lax.broadcasted_iota(jnp.int32, (modes, modes), 0)
    cols = lax.broadcasted_iota(jnp.int32, (modes, modes), 1)
    total = coupling[0].T + jnp.where(rows == cols, retain[0:1, :], 0.0)
    step = lax.broadcasted_iota(jnp.int32, (steps, modes), 0)
    state = jnp.zeros((steps, modes), F32)
    for t in range(steps):
        u = steps - 1 - t
        state = jnp.where(step == u, probe[...], state)
        state = state * retain[u : u + 1, :] + mm(split(state), split(coupling[u]))
        if t > 0:
            total = total * retain[t : t + 1, :] + mm(split(total), split(coupling[t]), True)
    whole[...] = total
    seen[...] = state


def drive_kernel(pos, arrived, retain, coupling, probe, shifted, kept, sent, seen):
    steps, modes = retain.shape
    sources, half, _ = arrived.shape
    n = sources * half
    samples = shifted.shape[0]
    loads = jnp.concatenate(
        [
            arrived[:, :, 0:modes].reshape(n, modes),
            arrived[:, :, modes : 2 * modes].reshape(n, modes),
        ],
        axis=0,
    )
    lh, ll = split(loads)
    codes = arrived[:, :, 2 * modes : 2 * modes + 128].reshape(n, 128).T
    codes = jnp.concatenate([codes[0:1, :], codes[1:2, :]], axis=1).astype(jnp.int32)
    place = lax.broadcasted_iota(jnp.int32, (samples, 2 * n), 0)
    lane = lax.broadcasted_iota(jnp.int32, (samples, 128), 1)
    shown = jnp.zeros((samples, 128), F32)
    field = None
    for t in range(steps):
        hit = jnp.where(place + t * samples == codes, 1.0, 0.0).astype(BF16)
        kick = dot(hit, lh) + dot(hit, ll)
        if t > 0:
            kick = kick + field * retain[t : t + 1, :] + mm(parts, split(coupling[t]), True)
        field = kick
        parts = split(field)
        shown = jnp.where(lane == t, jnp.sum(field * probe[...], axis=1, keepdims=True), shown)
    shifted[...] = field
    seen[...] = shown.T[:steps]
    c = pos[0]
    h = samples // 2

    @pl.when(c == 0)
    def _():
        kept[...] = field[:h]
        sent[...] = field[h:]

    @pl.when(c != 0)
    def _():
        kept[...] = field[h:]
        sent[...] = field[:h]


def pair_kernel(pos, mine, other, both, chip):
    c = pos[0]

    @pl.when(c == 0)
    def _():
        both[0] = mine[...]
        both[1] = other[...]

    @pl.when(c != 0)
    def _():
        both[0] = other[...]
        both[1] = mine[...]

    chip[...] = mm(split(both[0]), split(both[1]))


def order(place, count, ordered, refs):
    ordered[place] = refs[0][...]
    for s, ref in zip(SHIFTS, refs[1:]):
        ordered[lax.rem(place + count - s, count)] = ref[...]


def line_kernel(
    pos, a0, a1, a3, a2, b0, b2, b1, b3, prefix, line, before, packet, maps, shifts
):
    order(pos[1], NY, maps, (a0, a1, a3, a2))
    order(pos[1], NY, shifts, (b0, b1, b3, b2))
    total, moved = maps[0], shifts[0]
    for k in range(1, NY):
        prefix[k - 1] = total
        before[k - 1] = moved
        right = split(maps[k])
        total = mm(split(total), right)
        moved = mm(split(moved), right) + shifts[k]
    line[...] = total
    h = line.shape[0] // 2
    packet[:h] = line[pl.ds(pl.multiple_of(pos[0] * h, h), h), :]
    packet[h:] = moved


def group_kernel(
    pos,
    line,
    p0,
    p1,
    p3,
    p2,
    t1,
    t3,
    t2,
    prefix,
    before,
    through,
    high,
    low,
    b_through,
    b_group,
    maps,
    shifts,
    a_before,
    own,
):
    x = pos[2]
    modes = high.shape[0]
    h = modes // 2
    here = pl.ds(pl.multiple_of(pos[0] * h, h), h)
    there = pl.ds(pl.multiple_of((1 - pos[0]) * h, h), h)
    maps[x] = line[...]
    shifts[x] = p0[h:]
    for s, ref, theirs in zip(SHIFTS, (p1, p3, p2), (t1, t3, t2)):
        spot = lax.rem(x + NX - s, NX)
        maps[spot, here, :] = ref[:h]
        maps[spot, there, :] = theirs[:h]
        shifts[spot] = ref[h:]
    rows = lax.broadcasted_iota(jnp.int32, (modes, modes), 0)
    cols = lax.broadcasted_iota(jnp.int32, (modes, modes), 1)
    a_before[0] = jnp.where(rows == cols, 1.0, 0.0)
    own[0] = jnp.zeros_like(shifts[0])
    total, moved = maps[0], shifts[0]
    for k in range(1, NX):
        a_before[k] = total
        own[k] = moved
        right = split(maps[k])
        total = mm(split(total), right)
        moved = mm(split(moved), right) + shifts[k]
    high[...], low[...] = split(total)
    b_group[...] = moved
    through[0] = a_before[x]
    b_through[0] = own[x]
    a_own, b_own = split(a_before[x]), split(own[x])
    for k in range(1, NY):
        right = split(prefix[k - 1])
        through[k] = mm(a_own, right)
        b_through[k] = mm(b_own, right) + before[k - 1]


def pair_shift_kernel(pos, kept, got, both, first, s0, s1, s3, s2, chip):
    c = pos[0]
    y = pos[1]
    r = s0.shape[0]
    mine = kept[...]
    theirs = got[...]
    zero = jnp.where(c == 0, mine, theirs)
    one = jnp.where(c == 0, theirs, mine)
    first[...] = zero
    chip[...] = mm(split(zero), split(both[1])) + one
    for s, out in zip((0,) + SHIFTS, (s0, s1, s3, s2)):
        start = pl.multiple_of(lax.rem(y + s, NY) * r, r)
        out[...] = chip[pl.ds(start, r), :]


def released_rows(pos, initial, part):
    start = pl.multiple_of(pos[0] * (NY * part) + pos[1] * part, part)
    return initial[pl.ds(start, part), :]


def first_hop_kernel(pos, initial, high, low, shift, out):
    state = released_rows(pos, initial, out.shape[0])
    out[...] = mm(split(state), (high[...], low[...])) + shift[...]


def hop_kernel(pos, got, high, low, shift, out):
    out[...] = mm(split(got[...]), (high[...], low[...])) + shift[...]


def last_hop_kernel(pos, initial, *refs):
    gots, (maps, shifts, s0, s1, s3, s2, chips) = refs[:-7], refs[-7:]
    y = pos[1]
    g = pos[3]
    state = released_rows(pos, initial, s0.shape[0])
    for k, got in enumerate(gots):
        state = jnp.where(g == k + 1, got[...], state)
    group = split(state)
    for k in range(NY):
        chips[k] = mm(group, split(maps[k])) + shifts[k]
    for s, out in zip((0,) + SHIFTS, (s0, s1, s3, s2)):
        out[...] = chips[lax.rem(y + s, NY)]


def chip_kernel(pos, e0, e2, e1, e3, both, first, kept, sent, chip):
    c, y = pos[0], pos[1]
    r = e0.shape[0]
    for s, ref in zip((0,) + SHIFTS, (e0, e1, e3, e2)):
        start = pl.multiple_of(lax.rem(y + NY - s, NY) * r, r)
        chip[pl.ds(start, r), :] = ref[...]
    zero = chip[...]
    one = mm(split(zero), split(both[0])) + first[...]
    kept[...] = jnp.where(c == 0, zero, one)
    sent[...] = jnp.where(c == 0, one, zero)


def finish_kernel(pos, kept, got, whole, shifted, weights, driven, observed, final, start):
    c = pos[0]
    h = kept.shape[0]

    @pl.when(c == 0)
    def _():
        start[:h] = kept[...]
        start[h:] = got[...]

    @pl.when(c != 0)
    def _():
        start[:h] = got[...]
        start[h:] = kept[...]

    parts = split(start[...])
    final[...] = mm(parts, split(whole[...])) + shifted[...]
    observed[...] = mm(split(weights[...]), parts, True) + driven[...]


def body(initial_state, retain, coupling, probe, rec_sample, rec_step, rec_count, rec_load):
    steps, modes, _ = coupling.shape
    samples = initial_state.shape[0]
    owners, cap = rec_sample.shape[1:]
    half = samples // 2
    part = half // NY
    mat = (modes, modes)
    vm = lambda *s: pltpu.VMEM(s, F32)

    def at(x, y, c):
        return (x * NY + y) * 2 + c

    spots = [(x, y, c) for x in range(NX) for y in range(NY) for c in range(2)]
    swap = [(at(x, y, c), at(x, y, 1 - c)) for x, y, c in spots]

    def along_y(s):
        return [(at(x, y, c), at(x, (y + s) % NY, c)) for x, y, c in spots]

    def along_x(s):
        return [(at(x, y, c), at((x + s) % NX, y, c)) for x, y, c in spots]

    n_grp = lax.axis_size("grp")

    packed = pl.pallas_call(
        functools.partial(pack_kernel, samples=samples),
        out_shape=jax.ShapeDtypeStruct((owners, cap // 2, 2 * modes + 128), F32),
        in_specs=[pl.BlockSpec(memory_space=pltpu.HBM)] * 4,
        out_specs=pl.BlockSpec(memory_space=pltpu.VMEM),
        scratch_shapes=[
            pltpu.VMEM((cap, owners), jnp.int32),
            pltpu.VMEM((cap, owners), jnp.int32),
            pltpu.VMEM((1, owners), jnp.int32),
            pltpu.SemaphoreType.DMA((5,)),
        ],
        name="pack",
        cost_estimate=pl.CostEstimate(flops=3000000000, bytes_accessed=2**20, transcendentals=0),
    )(rec_load[0], rec_sample[0].T, rec_step[0].T, rec_count)
    arrived = lax.all_to_all(packed, "tm", split_axis=0, concat_axis=0)

    cube = 2 * modes * modes * modes
    probe_row = probe[None, :]
    whole, weights = call(
        compose_kernel,
        "compose",
        [mat, (steps, modes)],
        retain,
        coupling,
        probe_row,
        flops=22 * cube,
        after=(packed,),
    )
    other = lax.ppermute(whole, "tm", swap)
    both, chip = call(pair_kernel, "pair_map", [(2,) + mat, mat], whole, other, flops=3 * cube)
    chips = [lax.ppermute(chip, "tm", along_y(s)) for s in SHIFTS]
    shifted, kept, sent, driven = call(
        drive_kernel,
        "drive",
        [mat, (half, modes), (half, modes), (steps, samples)],
        arrived,
        retain,
        coupling,
        probe_row,
        flops=60 * cube,
    )
    back = lax.ppermute(sent, "tm", swap)
    small = (part, modes)
    first, *rows = call(
        pair_shift_kernel,
        "pair_shift",
        [(half, modes)] + [small] * 4,
        kept,
        back,
        both,
        scratch=[vm(half, modes)],
        flops=cube,
    )
    got = [lax.ppermute(r, "tm", along_y(s)) for r, s in zip(rows[1:], SHIFTS)]
    y_before, line, b_before, packet = call(
        line_kernel,
        "line",
        [(NY - 1,) + mat, mat, (NY - 1,) + small, (half + part, modes)],
        chip,
        *chips,
        rows[0],
        got[2],
        got[0],
        got[1],
        scratch=[vm(NY, *mat), vm(NY, *small)],
        flops=10 * cube,
    )
    packets = [lax.ppermute(packet, "tm", along_x(s)) for s in SHIFTS]
    swapped = [lax.ppermute(p, "tm", swap) for p in packets]
    half_mat = jax.ShapeDtypeStruct(mat, BF16)
    through, high, low, b_through, b_group = call(
        group_kernel,
        "group",
        [(NY,) + mat, half_mat, half_mat, (NY,) + small, small],
        line,
        packet,
        *packets,
        *swapped,
        y_before,
        b_before,
        scratch=[vm(NX, *mat), vm(NX, *small), vm(NX, *mat), vm(NX, *small)],
        flops=20 * cube,
    )
    (e,) = call(
        first_hop_kernel, "hop0", [small], initial_state, high, low, b_group, flops=cube
    )
    carried = [lax.ppermute(e, "grp", [(0, 1)])]
    for k in range(1, n_grp - 1):
        (e,) = call(hop_kernel, "hop", [small], carried[-1], high, low, b_group, flops=cube)
        carried.append(lax.ppermute(e, "grp", [(k, k + 1)]))
    rows = call(
        last_hop_kernel,
        "chips",
        [small] * 4,
        initial_state,
        *carried,
        through,
        b_through,
        scratch=[vm(NY, *small)],
        flops=2 * cube,
    )
    got = [lax.ppermute(r, "tm", along_y(s)) for r, s in zip(rows[1:], SHIFTS)]
    kept, sent = call(
        chip_kernel,
        "chip_start",
        [(half, modes)] * 2,
        rows[0],
        got[2],
        got[0],
        got[1],
        both,
        first,
        scratch=[vm(half, modes)],
        flops=cube,
    )
    back = lax.ppermute(sent, "tm", swap)
    observed, final = call(
        finish_kernel,
        "finish",
        [(steps, samples), mat],
        kept,
        back,
        whole,
        shifted,
        weights,
        driven,
        scratch=[vm(samples, modes)],
        flops=3 * cube,
    )
    return observed, final[None]


def solution(mesh):
    in_specs = (
        P(),
        P(("grp", "tm"), None),
        P(("grp", "tm"), None, None),
        P(),
        P(("grp", "tm"), None, None),
        P(("grp", "tm"), None, None),
        P(("grp", "tm"), None),
        P(("grp", "tm"), None, None, None),
    )
    out_specs = (P(("grp", "tm"), None), P(("grp", "tm"), None, None))
    return jax.shard_map(body, mesh=mesh, in_specs=in_specs, out_specs=out_specs, check_vma=False)
```
